512 devices in a mesh: rows: 64 (over z, x), cols: 8 (over y, core).
Axes of the slice: x: 4, y: 4, z: 16, core: 2. Of those that a mesh axis runs over, the one named last changes fastest.
Arguments:
- panel: float32 [2048, 32768], P('rows', 'cols'), may hold values from -0.03125 to 0.03125
- solved: float32 [32768, 64], P('cols'), may hold values from -6 to 6
- sketch: float32 [2048, 64], P('rows'), may hold values from -6 to 6
- inverses: float32 [2, 1024, 1024], P(None, 'rows', 'cols'), may hold values from -2 to 2, as said below
- coupling: float32 [1024, 1024], P('rows', 'cols'), may hold values from -0.1875 to 0.1875
- design: bfloat16 [131072, 2048], P('rows', 'cols'), may hold values from -0.125 to 0.125
- prior: float32 [131072, 64], P(('rows', 'cols')), may hold values from -6 to 6
Outputs:
- block_solution: float32 [2048, 64], P('rows')
- leverage: float32 [131072], P(('rows', 'cols'))
The draws below stay inside these ranges and needn't reach their ends.
Inputs may be any that keep to these rules, and one draw needn't show every extreme that they name: `inverses`: each of the two blocks is upper triangular with a positive diagonal.
All inputs are finite; a program needn't handle non-finite values.
Results may differ from the reference program's by a relative error of at most 0.00063.
Values sent between devices are 32-bit elements; how exact they have to be, the bound alone decides.
No kernel may reach another device: no remote copies, remote signals or barrier semaphores. Data moves between devices by JAX's collectives and lax.ppermute only.
A program may use at most 64 MiB of HBM per device.

```python
import jax
import jax.numpy as jnp
from jax import lax

K = 64
B = 1024
TAIL = 32768
MDEV = 2048
M = 131072
N_ROWS = 64


def draw_inverses(key, part):
    first, second = jax.random.split(jax.random.fold_in(key, 11))
    upper = jnp.clip(jax.random.normal(first, (2, B, B), jnp.float32), -4.0, 4.0)
    upper = upper / jnp.sqrt(jnp.float32(B))
    diagonal = jnp.exp(jax.random.uniform(second, (2, B), jnp.float32, -0.7, 0.4))
    index_row = jax.lax.broadcasted_iota(jnp.int32, (B, B), 0)
    index_col = jax.lax.broadcasted_iota(jnp.int32, (B, B), 1)
    strict = (index_col > index_row).astype(jnp.float32)
    same = (index_col == index_row).astype(jnp.float32)
    return upper * strict[None] + diagonal[:, :, None] * same[None]


def levels(stream_key, dims, shards, low, high):
    gain, own = 1.0, jax.random.fold_in(stream_key, 6)
    for axis_at, parts in shards:
        heights = jnp.exp(jax.random.uniform(jax.random.fold_in(own, axis_at), (parts,), jnp.float32, low / len(shards), high / len(shards)))
        gain = gain * jnp.repeat(heights, dims[axis_at] // parts).reshape([-1 if axis == axis_at else 1 for axis in range(len(dims))])
    return gain


def noise(key, dims, deviation, limit, pieces=(), held_as=jnp.bfloat16):
    values = deviation * jax.random.normal(key, dims, jnp.float32)
    if pieces:
        values = values * levels(key, dims, pieces, -0.22, 0.18)
    return jnp.clip(values, -limit, limit).astype(held_as)


def setup_inputs(seed: int = 0) -> dict:
    key_of = jax.random.split(jax.random.key(seed), 8)
    return {
        "panel": noise(key_of[0], (2 * B, TAIL), TAIL ** -0.5, 0.03125, ((0, 64), (1, 8)), jnp.float32),
        "solved": noise(key_of[1], (TAIL, K), 1.0, 6.0, ((0, 8),), jnp.float32),
        "sketch": noise(key_of[2], (2 * B, K), 1.0, 6.0, ((0, 64),), jnp.float32),
        "inverses": draw_inverses(jax.random.fold_in(key_of[7], 71), 0),
        "coupling": noise(key_of[4], (B, B), B ** -0.5, 0.1875, ((0, 64), (1, 8)), jnp.float32),
        "design": noise(key_of[5], (M, 2 * B), (2 * B) ** -0.5, 0.125, ((0, 64), (1, 8))),
        "prior": noise(key_of[6], (M, K), 1.0, 6.0, ((0, 512),), jnp.float32),
    }


def reference(panel, solved, sketch, inverses, coupling, design, prior):
    highest = lax.Precision.HIGHEST
    right = sketch - jnp.dot(panel, solved, precision=highest)
    y_last = jnp.dot(inverses[1], right[B:], precision=highest)
    bent = jnp.dot(coupling, y_last, precision=highest)
    y_first = jnp.dot(inverses[0], right[:B] - bent, precision=highest)
    block_solution = jnp.concatenate([y_first, y_last], axis=0)
    rounded = block_solution.astype(jnp.bfloat16).astype(jnp.float32)
    stacked = design.reshape(N_ROWS, MDEV, 2 * B)

    def one_block(rows_block):
        return jnp.dot(rows_block.astype(jnp.float32), rounded, precision=highest)

    product = prior + lax.map(one_block, stacked).reshape(N_ROWS * MDEV, K)
    leverage = jnp.mean(product * product, axis=1)
    return block_solution, leverage
```

```python
import jax
import jax.numpy as jnp
from jax import lax
from jax.sharding import Mesh
from jax.sharding import PartitionSpec as P

HIGHEST = lax.Precision.HIGHEST


def dot(a, b):
    return jnp.dot(a, b, precision=HIGHEST)


def exchange(value, axes):
    return lax.all_to_all(value, axes, 0, 0, tiled=True)


def to_all(value, axes, count):
    return exchange(jnp.broadcast_to(value[None], (count, *value.shape)), axes)


def packed(value):
    half = value.shape[-2] // 2
    return jnp.concatenate([value[..., :half, :], value[..., half:, :]], axis=-1)


def unpacked(value):
    return jnp.concatenate([value[..., :64], value[..., 64:]], axis=-2)


def local(panel, solved, sketch, inverses, coupling, design, prior):
    zh, zl, x, c = (lax.axis_index(name) for name in ("zh", "zl", "x", "c"))

    start = jnp.where(c == 0, sketch, 0.0) - dot(panel, solved)
    rows = start.reshape(8, 2, 128)

    def by_subset(block):
        return block.reshape(16, 4, 8, 4).transpose(2, 0, 1, 3).reshape(8, 2, 128)

    pieces = jnp.concatenate([rows, by_subset(inverses[1]), by_subset(inverses[0])], axis=1)
    turned = coupling.reshape(4, 4, 2, 4, 16).transpose(3, 0, 1, 2, 4).reshape(4, 1, 4, 1, 128)
    message = jnp.concatenate(
        [
            jnp.broadcast_to(pieces[None], (4, 8, 6, 128)),
            jnp.broadcast_to(turned, (4, 2, 4, 1, 128)).reshape(4, 8, 1, 128),
        ],
        axis=2,
    )
    got = exchange(message.reshape(32, 7, 128), ("x", "c")).reshape(4, 8, 7, 128)
    right = got[:, :, :2].sum(axis=1).reshape(16, 64)
    mine = lax.dynamic_index_in_dim(got, x, 0, keepdims=False)

    def joined(block):
        return block.reshape(8, 16, 16).transpose(1, 0, 2).reshape(16, 128)

    last_rows = joined(mine[:, 2:4])
    first_rows = joined(mine[:, 4:6])
    turned = lax.dynamic_index_in_dim(
        got[:, :, 6].reshape(2, 2, 8, 128), c // 4, 1, keepdims=False
    )
    turned = turned.reshape(2, 8, 4, 2, 2, 8).transpose(4, 0, 2, 1, 3, 5).reshape(2, 8, 128)

    common = packed(right)
    message = jnp.stack(
        [
            jnp.concatenate([common, last_rows[8 * h : 8 * h + 8], turned[h], first_rows])
            for h in range(2)
        ]
    )
    message = jnp.broadcast_to(message[None], (8, 2, 40, 128)).reshape(16, 40, 128)
    got = exchange(message, ("zh", "zl"))
    right = unpacked(got[:, :8])
    right_first = right[:8].reshape(128, 64)
    right_last = right[8:].reshape(128, 64)
    inverse_last = got[:, 8:16].reshape(128, 128)
    couple = got[:, 16:24].reshape(128, 128)
    inverse_first = got[:, 24:40].reshape(256, 128)

    parts = to_all(packed(dot(inverse_last, right_last)), "c", 8)
    y_last = unpacked(parts.sum(axis=0))

    bent = packed(dot(couple, y_last))
    piece = packed(lax.dynamic_slice_in_dim(y_last, 32 * (c % 4), 32, 0))
    parts = to_all(jnp.concatenate([bent, piece]), ("zl", "x"), 8)
    bent = unpacked(parts[:, :64].sum(axis=0))
    block_last = unpacked(parts[:, 64:]).reshape(2, 4, 4, 8, 64)
    block_last = block_last.transpose(2, 1, 0, 3, 4).reshape(256, 64)

    terms = packed(dot(inverse_first, right_first - bent).reshape(4, 64, 64))
    terms = jnp.broadcast_to(terms[None], (8, 4, 32, 128)).reshape(32, 32, 128)
    parts = exchange(terms, ("x", "c")).reshape(4, 8, 32, 128)
    block_first = unpacked(parts.sum(axis=1)).reshape(4, 4, 16, 64)
    block_first = block_first.transpose(1, 0, 2, 3).reshape(256, 64)
    block = jnp.where(c < 4, block_first, block_last)

    rounded = block.astype(jnp.bfloat16)
    product = jnp.dot(design, rounded, preferred_element_type=jnp.float32)
    product = packed(product.reshape(8, 256, 64))
    own = packed(lax.dynamic_slice_in_dim(block, 32 * (4 * zl + x), 32, 0))
    message = jnp.concatenate(
        [product, jnp.broadcast_to(own[None], (8, 16, 128))], axis=1
    )
    got = exchange(message, "c")
    block_solution = unpacked(lax.dynamic_index_in_dim(got, zh, 0, keepdims=False)[128:])
    total = packed(prior) + got[:, :128].sum(axis=0)
    leverage = (total * total).reshape(128, 2, 64).sum(axis=2).T.reshape(256) * (1.0 / 64)
    return block_solution, leverage


def solution(mesh):
    fine = Mesh(mesh.devices.reshape(8, 2, 4, 8), ("zh", "zl", "x", "c"))
    r = ("zh", "zl", "x")
    in_specs = (
        P(r, "c"),
        P("c", None),
        P(r, None),
        P(None, r, "c"),
        P(r, "c"),
        P(r, "c"),
        P((*r, "c"), None),
    )
    out_specs = (P(r, None), P((*r, "c")))
    return jax.shard_map(local, mesh=fine, in_specs=in_specs, out_specs=out_specs, check_vma=False)
```

```python
import jax
import jax.numpy as jnp
from jax import lax
from jax.sharding import Mesh
from jax.sharding import PartitionSpec as P

HIGHEST = lax.Precision.HIGHEST


def dot(a, b):
    return jnp.dot(a, b, precision=HIGHEST)


def exchange(value, axes):
    return lax.all_to_all(value, axes, 0, 0, tiled=True)


def to_all(value, axes, count):
    return exchange(jnp.broadcast_to(value[None], (count, *value.shape)), axes)


def packed(value):
    half = value.shape[-2] // 2
    return jnp.concatenate([value[..., :half, :], value[..., half:, :]], axis=-1)


def unpacked(value):
    return jnp.concatenate([value[..., :64], value[..., 64:]], axis=-2)


def local(panel, solved, sketch, inverses, coupling, design, prior):
    zh, zl, x, c = (lax.axis_index(name) for name in ("zh", "zl", "x", "c"))

    start = jnp.where(c == 0, sketch, 0.0) - dot(panel, solved)
    rows = start.reshape(8, 2, 128)

    def by_subset(block):
        return block.reshape(16, 4, 8, 4).transpose(2, 0, 1, 3).reshape(8, 2, 128)

    pieces = jnp.concatenate([rows, by_subset(inverses[1]), by_subset(inverses[0])], axis=1)
    turned = coupling.reshape(4, 4, 2, 4, 16).transpose(3, 0, 1, 2, 4).reshape(4, 1, 4, 1, 128)
    message = jnp.concatenate(
        [
            jnp.broadcast_to(pieces[None], (4, 8, 6, 128)),
            jnp.broadcast_to(turned, (4, 2, 4, 1, 128)).reshape(4, 8, 1, 128),
        ],
        axis=2,
    )
    got = exchange(message.reshape(32, 7, 128), ("x", "c")).reshape(4, 8, 7, 128)
    right = got[:, :, :2].sum(axis=1).reshape(16, 64)
    mine = lax.dynamic_index_in_dim(got, x, 0, keepdims=False)

    def joined(block):
        return block.reshape(8, 16, 16).transpose(1, 0, 2).reshape(16, 128)

    last_rows = joined(mine[:, 2:4])
    first_rows = joined(mine[:, 4:6])
    turned = lax.dynamic_index_in_dim(
        got[:, :, 6].reshape(2, 2, 8, 128), c // 4, 1, keepdims=False
    )
    turned = turned.reshape(2, 8, 4, 2, 2, 8).transpose(4, 0, 2, 1, 3, 5).reshape(16, 128)

    common = packed(right)
    message = jnp.stack(
        [
            jnp.concatenate([common, *(m[8 * h : 8 * h + 8] for m in (last_rows, turned, first_rows))])
            for h in range(2)
        ]
    )
    message = jnp.broadcast_to(message[None], (8, 2, 32, 128)).reshape(16, 32, 128)
    got = exchange(message, ("zh", "zl"))
    right = unpacked(got[:, :8])
    right_first = right[:8].reshape(128, 64)
    right_last = right[8:].reshape(128, 64)
    inverse_last = got[:, 8:16].reshape(128, 128)
    couple = got[:, 16:24].reshape(128, 128)
    inverse_first = got[:, 24:32].reshape(128, 128)

    parts = to_all(packed(dot(inverse_last, right_last)), "c", 8)
    y_last = unpacked(parts.sum(axis=0))

    bent = packed(dot(couple, y_last))
    piece = packed(lax.dynamic_slice_in_dim(y_last, 32 * (c % 4), 32, 0))
    parts = to_all(jnp.concatenate([bent, piece]), ("zl", "x"), 8)
    bent = unpacked(parts[:, :64].sum(axis=0))
    block_last = unpacked(parts[:, 64:]).reshape(2, 4, 4, 8, 64)
    block_last = block_last.transpose(2, 1, 0, 3, 4).reshape(256, 64)

    terms = packed(dot(inverse_first, right_first - bent).reshape(4, 32, 64))
    terms = jnp.broadcast_to(terms[None], (16, 4, 16, 128)).reshape(64, 16, 128)
    parts = exchange(terms, ("zl", "x", "c")).reshape(2, 4, 8, 16, 128)
    block_first = unpacked(parts.sum(axis=2)).reshape(2, 4, 4, 8, 64)
    block_first = block_first.transpose(2, 1, 0, 3, 4).reshape(256, 64)
    block = jnp.where(c < 4, block_first, block_last)

    rounded = block.astype(jnp.bfloat16)
    product = jnp.dot(design, rounded, preferred_element_type=jnp.float32)
    product = packed(product.reshape(8, 256, 64))
    own = packed(lax.dynamic_slice_in_dim(block, 32 * (4 * zl + x), 32, 0))
    message = jnp.concatenate(
        [product, jnp.broadcast_to(own[None], (8, 16, 128))], axis=1
    )
    got = exchange(message, "c")
    block_solution = unpacked(lax.dynamic_index_in_dim(got, zh, 0, keepdims=False)[128:])
    total = packed(prior) + got[:, :128].sum(axis=0)
    leverage = (total * total).reshape(128, 2, 64).sum(axis=2).T.reshape(256) * (1.0 / 64)
    return block_solution, leverage


def solution(mesh):
    fine = Mesh(mesh.devices.reshape(8, 2, 4, 8), ("zh", "zl", "x", "c"))
    r = ("zh", "zl", "x")
    in_specs = (
        P(r, "c"),
        P("c", None),
        P(r, None),
        P(None, r, "c"),
        P(r, "c"),
        P(r, "c"),
        P((*r, "c"), None),
    )
    out_specs = (P(r, None), P((*r, "c")))
    return jax.shard_map(local, mesh=fine, in_specs=in_specs, out_specs=out_specs, check_vma=False)
```

```python
import jax
import jax.numpy as jnp
from jax import lax
from jax.experimental import pallas as pl
from jax.experimental.pallas import tpu as pltpu
from jax.sharding import Mesh
from jax.sharding import PartitionSpec as P

HIGHEST = lax.Precision.HIGHEST
VMEM = pl.BlockSpec(memory_space=pltpu.VMEM)
SMEM = pl.BlockSpec(memory_space=pltpu.SMEM)
NT = (((1,), (1,)), ((), ()))


def dot(a, b):
    return jnp.dot(a, b, precision=HIGHEST, preferred_element_type=jnp.float32)


def exchange(value, axes):
    return lax.all_to_all(value, axes, 0, 0, tiled=True)


def packed(value):
    half = value.shape[-2] // 2
    return jnp.concatenate([value[..., :half, :], value[..., half:, :]], axis=-1)


def unpacked(value):
    return jnp.concatenate([value[..., :64], value[..., 64:]], axis=-2)


def call(body, out, *args, specs=None, scratch=(), limit=32 << 20):
    return pl.pallas_call(
        body,
        out_shape=out,
        in_specs=specs or [VMEM] * len(args),
        out_specs=jax.tree.map(lambda _: VMEM, out),
        scratch_shapes=scratch,
        compiler_params=pltpu.CompilerParams(vmem_limit_bytes=limit),
    )(*args)


def f32(*shape):
    return jax.ShapeDtypeStruct(shape, jnp.float32)


def two_parts(value):
    high = value.astype(jnp.bfloat16)
    low = (value - high.astype(jnp.float32)).astype(jnp.bfloat16)
    return jnp.concatenate([high, low], axis=0)


def panel_body(column, panel, solved_t, sketch, out):
    products = lax.dot_general(
        two_parts(panel[...]), two_parts(solved_t[...]), NT, preferred_element_type=jnp.float32
    )
    total = products[:32] + products[32:]
    total = total[:, :64] + total[:, 64:]
    out[...] = jnp.where(column[0] == 0, sketch[...], 0.0) - total


def last_body(got, out):
    right = unpacked(got[8:16, 0:8].reshape(64, 128))
    terms = packed(dot(got[:, 8:16].reshape(128, 128), right))
    for k in range(8):
        out[k] = terms


def bent_body(where, parts, got, out, held):
    y_last = unpacked(parts[...].sum(axis=0))
    held[...] = y_last
    bent = dot(got[:, 16:24].reshape(128, 128), y_last).reshape(8, 2, 8, 64)
    bent = jnp.concatenate([bent[:, 0].reshape(64, 64), bent[:, 1].reshape(64, 64)], axis=1)
    piece = packed(held[pl.ds(pl.multiple_of(where[0], 32), 32), :])
    for k in range(8):
        out[k, :64] = bent
        out[k, 64:] = piece


def first_body(parts, got, out):
    bent = parts[:, :64].sum(axis=0)
    right = unpacked(got[0:8, 0:8].reshape(64, 128) - bent)
    terms = dot(got[:, 24:32].reshape(128, 128), right)
    for g in range(4):
        piece = packed(terms[32 * g : 32 * g + 32])
        for k in range(16):
            out[4 * k + g] = piece


def design_body(where, first, last, design, out, held):
    for h in range(2):
        for x in range(4):
            k = 4 * h + x
            piece = first[8 * k : 8 * k + 8].sum(axis=0)
            piece = jnp.where(where[0] < 4, piece, last[k, 64:80])
            for z in range(4):
                row = 64 * z + 16 * x + 8 * h
                held[row : row + 8, :] = piece[
                    8 * (z % 2) : 8 * (z % 2) + 8, 64 * (z // 2) : 64 * (z // 2) + 64
                ]
    turned = held[...].T.astype(jnp.bfloat16)
    own = held[pl.ds(pl.multiple_of(where[1], 32), 32), :]
    own = jnp.concatenate([own[8 * k : 8 * k + 8] for k in range(4)], axis=1)
    for k in range(8):
        out[k, :64] = lax.dot_general(
            turned, design[256 * k : 256 * k + 256], NT, preferred_element_type=jnp.float32
        )
        out[k, 64:] = own


def leverage_body(where, got, prior_t, solution_rows, leverage):
    total = prior_t[...] + got[:, :64].sum(axis=0)
    leverage[...] = jnp.sum(total * total, axis=0, keepdims=True) * (1.0 / 64)
    own = got[where[0], 64:72]
    for k in range(4):
        solution_rows[8 * k : 8 * k + 8, :] = own[:, 64 * k : 64 * k + 64]


def local(panel, solved, sketch, inverses, coupling, design, prior):
    zh, zl, x, c = (lax.axis_index(name) for name in ("zh", "zl", "x", "c"))

    start = call(
        panel_body,
        f32(32, 64),
        c.reshape(1),
        panel,
        solved.T,
        sketch,
        specs=[SMEM, VMEM, VMEM, VMEM],
    )
    rows = start.reshape(8, 2, 128)

    def by_subset(block):
        return block.reshape(16, 4, 8, 4).transpose(2, 0, 1, 3).reshape(8, 2, 128)

    pieces = jnp.concatenate([rows, by_subset(inverses[1]), by_subset(inverses[0])], axis=1)
    turned = coupling.reshape(4, 4, 2, 4, 16).transpose(3, 0, 1, 2, 4).reshape(4, 1, 4, 1, 128)
    message = jnp.concatenate(
        [
            jnp.broadcast_to(pieces[None], (4, 8, 6, 128)),
            jnp.broadcast_to(turned, (4, 2, 4, 1, 128)).reshape(4, 8, 1, 128),
        ],
        axis=2,
    )
    got = exchange(message.reshape(32, 7, 128), ("x", "c")).reshape(4, 8, 7, 128)
    right = got[:, :, :2].sum(axis=1).reshape(16, 64)
    mine = lax.dynamic_index_in_dim(got, x, 0, keepdims=False)

    def joined(block):
        return block.reshape(8, 16, 2, 8).transpose(1, 2, 0, 3).reshape(16, 128)

    last_rows = joined(mine[:, 2:4])
    first_rows = joined(mine[:, 4:6])
    turned = lax.dynamic_index_in_dim(
        got[:, :, 6].reshape(2, 2, 8, 128), c // 4, 1, keepdims=False
    )
    turned = turned.reshape(2, 8, 4, 2, 2, 8).transpose(4, 0, 2, 1, 3, 5).reshape(16, 128)

    common = packed(right)
    message = jnp.stack(
        [
            jnp.concatenate([common, *(m[8 * h : 8 * h + 8] for m in (last_rows, turned, first_rows))])
            for h in range(2)
        ]
    )
    message = jnp.broadcast_to(message[None], (8, 2, 32, 128)).reshape(16, 32, 128)
    got = exchange(message, ("zh", "zl"))

    parts = exchange(call(last_body, f32(8, 64, 128), got), "c")

    last = exchange(
        call(
            bent_body,
            f32(8, 80, 128),
            (32 * (c % 4)).reshape(1),
            parts,
            got,
            specs=[SMEM, VMEM, VMEM],
            scratch=[pltpu.VMEM((128, 64), jnp.float32)],
        ),
        ("zl", "x"),
    )

    first = exchange(call(first_body, f32(64, 16, 128), last, got), ("zl", "x", "c"))

    message = call(
        design_body,
        f32(8, 72, 256),
        jnp.stack([c, 32 * (4 * zl + x)]),
        first,
        last,
        design,
        specs=[SMEM, VMEM, VMEM, VMEM],
        scratch=[pltpu.VMEM((256, 64), jnp.float32)],
    )
    got = exchange(message, "c")
    block_solution, leverage = call(
        leverage_body,
        (f32(32, 64), f32(1, 256)),
        zh.reshape(1),
        got,
        prior.T,
        specs=[SMEM, VMEM, VMEM],
    )
    return block_solution, leverage.reshape(256)


def solution(mesh):
    fine = Mesh(mesh.devices.reshape(8, 2, 4, 8), ("zh", "zl", "x", "c"))
    r = ("zh", "zl", "x")
    in_specs = (
        P(r, "c"),
        P("c", None),
        P(r, None),
        P(None, r, "c"),
        P(r, "c"),
        P(r, "c"),
        P((*r, "c"), None),
    )
    out_specs = (P(r, None), P((*r, "c")))
    return jax.shard_map(local, mesh=fine, in_specs=in_specs, out_specs=out_specs, check_vma=False)
```

```python
import jax
import jax.numpy as jnp
from jax import lax
from jax.experimental import pallas as pl
from jax.experimental.pallas import tpu as pltpu
from jax.sharding import Mesh
from jax.sharding import PartitionSpec as P

HIGHEST = lax.Precision.HIGHEST
VMEM = pl.BlockSpec(memory_space=pltpu.VMEM)
SMEM = pl.BlockSpec(memory_space=pltpu.SMEM)
NT = (((1,), (1,)), ((), ()))


def dot(a, b):
    return jnp.dot(a, b, precision=HIGHEST, preferred_element_type=jnp.float32)


def exchange(value, axes):
    return lax.all_to_all(value, axes, 0, 0, tiled=True)


def packed(value):
    half = value.shape[-2] // 2
    return jnp.concatenate([value[..., :half, :], value[..., half:, :]], axis=-1)


def unpacked(value):
    return jnp.concatenate([value[..., :64], value[..., 64:]], axis=-2)


def call(body, out, *args, specs=None, scratch=(), limit=32 << 20):
    return pl.pallas_call(
        body,
        out_shape=out,
        in_specs=specs or [VMEM] * len(args),
        out_specs=jax.tree.map(lambda _: VMEM, out),
        scratch_shapes=scratch,
        compiler_params=pltpu.CompilerParams(vmem_limit_bytes=limit),
    )(*args)


def f32(*shape):
    return jax.ShapeDtypeStruct(shape, jnp.float32)


def two_parts(value):
    high = value.astype(jnp.bfloat16)
    low = (value - high.astype(jnp.float32)).astype(jnp.bfloat16)
    return jnp.concatenate([high, low], axis=0)


def permuted(value, source_of):
    row = lax.broadcasted_iota(jnp.int32, (128, 128), 0)
    lane = lax.broadcasted_iota(jnp.int32, (128, 128), 1)
    return dot(value, (row == source_of(lane)).astype(jnp.float32))


def staggered(value, step, shift=0):
    row = lax.broadcasted_iota(jnp.int32, value.shape, 0) % (128 // (step % 128 & -(step % 128)))
    out = value
    for i in range(128 // (step % 128 & -(step % 128))):
        turn = (shift + step * i) % 128
        out = jnp.where(row == i, pltpu.roll(value, turn, 1) if turn else value, out)
    return out


def start_body(column, panel_hbm, solved_hbm, sketch_hbm, inverses_hbm, coupling_hbm, out, *held):
    sources = (inverses_hbm, coupling_hbm, panel_hbm, solved_hbm, sketch_hbm)
    inverses, coupling, panel, solved_t, sketch, sems = held
    copies = [
        pltpu.make_async_copy(source, target, sems.at[k])
        for k, (source, target) in enumerate(zip(sources, held))
    ]
    for copy in copies:
        copy.start()

    copies[0].wait()
    both = jnp.concatenate([inverses[1], inverses[0]], axis=0)
    both = permuted(both, lambda m: 32 * (m % 16 // 4) + 4 * (m // 16) + m % 4)
    both = staggered(both, 16)
    group = lax.broadcasted_iota(jnp.int32, (32, 128), 1) // 16
    row = lax.broadcasted_iota(jnp.int32, (32, 128), 0)
    for c2 in range(8):
        kept = jnp.where(group == (c2 + row) % 8, both, 0.0)
        kept = kept.reshape(4, 8, 128).sum(axis=1)
        for x2 in range(4):
            out[8 * x2 + c2, 2:6] = kept

    copies[1].wait()
    couple = permuted(
        coupling[...], lambda m: 64 * (m % 16 // 8) + 16 * (m // 32) + 8 * (m % 32 // 16) + m % 8
    )
    couple = staggered(couple, 32)
    group = group[:16] // 2
    row = row[:16]
    for x2 in range(4):
        kept = jnp.where(group == (x2 + row) % 4, couple, 0.0)
        for g in range(4):
            piece = jnp.sum(jnp.where(row // 4 == g, kept, 0.0), axis=0, keepdims=True)
            out[8 * x2 + g, 6:7] = piece
            out[8 * x2 + 4 + g, 6:7] = piece
            out[8 * x2 + g, 7:8] = piece
            out[8 * x2 + 4 + g, 7:8] = piece

    for copy in copies[2:]:
        copy.wait()
    products = lax.dot_general(
        two_parts(panel[...]), two_parts(solved_t[...]), NT, preferred_element_type=jnp.float32
    )
    total = products[:32] + products[32:]
    total = total[:, :64] + total[:, 64:]
    total = jnp.where(column[0] == 0, sketch[...], 0.0) - total
    for c2 in range(8):
        piece = packed(total[4 * c2 : 4 * c2 + 4])
        for x2 in range(4):
            out[8 * x2 + c2, 0:2] = piece


def split_body(where, got, out):
    x, c = where[0], where[1]
    right = [unpacked(got[8 * k : 8 * k + 8, 0:2].sum(axis=0)) for k in range(4)]
    right = jnp.concatenate(
        [jnp.concatenate(right[:2], axis=0), jnp.concatenate(right[2:], axis=0)], axis=1
    )
    group = lax.broadcasted_iota(jnp.int32, (8, 128), 1) // 16
    row = lax.broadcasted_iota(jnp.int32, (8, 128), 0)

    mats = [jnp.zeros((8, 128), jnp.float32) for _ in range(4)]
    for c1 in range(8):
        piece = got[8 * x + c1, 2:6]
        piece = pltpu.roll(piece, (16 * (c1 + 8) - 16 * c) % 128, 1)
        for k in range(4):
            mats[k] = jnp.where(group == (c1 + row) % 8, piece[k : k + 1], mats[k])
    mats = [staggered(mat, -16) for mat in mats]

    halves = [jnp.zeros((8, 128), jnp.float32) for _ in range(2)]
    for a in range(2):
        for c1 in range(8):
            piece = got[8 * (c // 4 + 2 * a) + c1, 6:8]
            piece = pltpu.roll(piece, (16 * c1 + 128 - 32 * x) % 128, 1)[:1]
            for h in range(2):
                here = (group == (2 * row + h + c1) % 8) & (row // 4 == a)
                halves[h] = jnp.where(here, piece, halves[h])
    halves = [staggered(half, -32, -16 * h) for h, half in enumerate(halves)]

    for k in range(8):
        for h in range(2):
            out[2 * k + h, 0:8] = right
            out[2 * k + h, 8:16] = mats[h]
            out[2 * k + h, 16:24] = halves[h]
            out[2 * k + h, 24:32] = mats[2 + h]


def last_body(got, out):
    right = unpacked(got[8:16, 0:8]).reshape(128, 64)
    terms = packed(dot(got[:, 8:16].reshape(128, 128), right))
    for k in range(8):
        out[k] = terms


def bent_body(where, parts, got, out, held):
    y_last = unpacked(parts[...].sum(axis=0))
    held[...] = y_last
    bent = dot(got[:, 16:24].reshape(128, 128), y_last).reshape(8, 2, 8, 64)
    bent = jnp.concatenate([bent[:, 0].reshape(64, 64), bent[:, 1].reshape(64, 64)], axis=1)
    piece = packed(held[pl.ds(pl.multiple_of(where[0], 32), 32), :])
    for k in range(8):
        out[k, :64] = bent
        out[k, 64:] = piece


def first_body(parts, got, out):
    bent = parts[:, :64].sum(axis=0)
    right = unpacked(got[0:8, 0:8] - bent.reshape(8, 8, 128)).reshape(128, 64)
    terms = dot(got[:, 24:32].reshape(128, 128), right)
    for g in range(4):
        piece = packed(terms[32 * g : 32 * g + 32])
        for k in range(16):
            out[4 * k + g] = piece


def design_body(where, first, last, design, out, held):
    for h in range(2):
        for x in range(4):
            k = 4 * h + x
            piece = first[8 * k : 8 * k + 8].sum(axis=0)
            piece = jnp.where(where[0] < 4, piece, last[k, 64:80])
            for z in range(4):
                row = 64 * z + 16 * x + 8 * h
                held[row : row + 8, :] = piece[
                    8 * (z % 2) : 8 * (z % 2) + 8, 64 * (z // 2) : 64 * (z // 2) + 64
                ]
    turned = held[...].T.astype(jnp.bfloat16)
    own = held[pl.ds(pl.multiple_of(where[1], 32), 32), :]
    own = jnp.concatenate([own[8 * k : 8 * k + 8] for k in range(4)], axis=1)
    for k in range(8):
        out[k, :64] = lax.dot_general(
            turned, design[256 * k : 256 * k + 256], NT, preferred_element_type=jnp.float32
        )
        out[k, 64:] = own


def leverage_body(where, got, prior_t, solution_rows, leverage):
    total = prior_t[...] + got[:, :64].sum(axis=0)
    leverage[...] = jnp.sum(total * total, axis=0, keepdims=True) * (1.0 / 64)
    own = got[where[0], 64:72]
    for k in range(4):
        solution_rows[8 * k : 8 * k + 8, :] = own[:, 64 * k : 64 * k + 64]


def local(panel, solved, sketch, inverses, coupling, design, prior):
    zh, zl, x, c = (lax.axis_index(name) for name in ("zh", "zl", "x", "c"))

    message = call(
        start_body,
        f32(32, 8, 128),
        c.reshape(1),
        panel,
        solved.T,
        sketch,
        inverses,
        coupling,
        specs=[SMEM] + [pl.BlockSpec(memory_space=pl.ANY)] * 5,
        scratch=[
            pltpu.VMEM((2, 16, 128), jnp.float32),
            pltpu.VMEM((16, 128), jnp.float32),
            pltpu.VMEM((32, 4096), jnp.float32),
            pltpu.VMEM((64, 4096), jnp.float32),
            pltpu.VMEM((32, 64), jnp.float32),
            pltpu.SemaphoreType.DMA((5,)),
        ],
    )
    got = exchange(message, ("x", "c"))

    message = call(split_body, f32(16, 32, 128), jnp.stack([x, c]), got, specs=[SMEM, VMEM])
    got = exchange(message, ("zh", "zl"))

    parts = exchange(call(last_body, f32(8, 64, 128), got), "c")

    last = exchange(
        call(
            bent_body,
            f32(8, 80, 128),
            (32 * (c % 4)).reshape(1),
            parts,
            got,
            specs=[SMEM, VMEM, VMEM],
            scratch=[pltpu.VMEM((128, 64), jnp.float32)],
        ),
        ("zl", "x"),
    )

    first = exchange(call(first_body, f32(64, 16, 128), last, got), ("zl", "x", "c"))

    message = call(
        design_body,
        f32(8, 72, 256),
        jnp.stack([c, 32 * (4 * zl + x)]),
        first,
        last,
        design,
        specs=[SMEM, VMEM, VMEM, VMEM],
        scratch=[pltpu.VMEM((256, 64), jnp.float32)],
    )
    got = exchange(message, "c")
    block_solution, leverage = call(
        leverage_body,
        (f32(32, 64), f32(1, 256)),
        zh.reshape(1),
        got,
        prior.T,
        specs=[SMEM, VMEM, VMEM],
    )
    return block_solution, leverage.reshape(256)


def solution(mesh):
    fine = Mesh(mesh.devices.reshape(8, 2, 4, 8), ("zh", "zl", "x", "c"))
    r = ("zh", "zl", "x")
    in_specs = (
        P(r, "c"),
        P("c", None),
        P(r, None),
        P(None, r, "c"),
        P(r, "c"),
        P(r, "c"),
        P((*r, "c"), None),
    )
    out_specs = (P(r, None), P((*r, "c")))
    return jax.shard_map(local, mesh=fine, in_specs=in_specs, out_specs=out_specs, check_vma=False)
```

```python
import jax
import jax.numpy as jnp
from jax import lax
from jax.experimental import pallas as pl
from jax.experimental.pallas import tpu as pltpu
from jax.sharding import Mesh
from jax.sharding import PartitionSpec as P

HIGHEST = lax.Precision.HIGHEST
VMEM = pl.BlockSpec(memory_space=pltpu.VMEM)
SMEM = pl.BlockSpec(memory_space=pltpu.SMEM)
NT = (((1,), (1,)), ((), ()))


def dot(a, b):
    return jnp.dot(a, b, precision=HIGHEST, preferred_element_type=jnp.float32)


def exchange(value, axes):
    return lax.all_to_all(value, axes, 0, 0, tiled=True)


def packed(value):
    half = value.shape[-2] // 2
    return jnp.concatenate([value[..., :half, :], value[..., half:, :]], axis=-1)


def unpacked(value):
    return jnp.concatenate([value[..., :64], value[..., 64:]], axis=-2)


def call(body, out, *args, specs=None, scratch=(), limit=32 << 20):
    return pl.pallas_call(
        body,
        out_shape=out,
        in_specs=specs or [VMEM] * len(args),
        out_specs=jax.tree.map(lambda _: VMEM, out),
        scratch_shapes=scratch,
        compiler_params=pltpu.CompilerParams(vmem_limit_bytes=limit),
    )(*args)


def f32(*shape):
    return jax.ShapeDtypeStruct(shape, jnp.float32)


def two_parts(value):
    high = value.astype(jnp.bfloat16)
    low = (value - high.astype(jnp.float32)).astype(jnp.bfloat16)
    return jnp.concatenate([high, low], axis=0)


def permuted(value, source_of):
    row = lax.broadcasted_iota(jnp.int32, (128, 128), 0)
    lane = lax.broadcasted_iota(jnp.int32, (128, 128), 1)
    return dot(value, (row == source_of(lane)).astype(jnp.float32))


def staggered(value, step, shift=0):
    row = lax.broadcasted_iota(jnp.int32, value.shape, 0) % (128 // (step % 128 & -(step % 128)))
    out = value
    for i in range(128 // (step % 128 & -(step % 128))):
        turn = (shift + step * i) % 128
        out = jnp.where(row == i, pltpu.roll(value, turn, 1) if turn else value, out)
    return out


def start_body(where, panel_hbm, solved_hbm, sketch_hbm, inverses_hbm, coupling_hbm, out, *held):
    sources = (inverses_hbm, coupling_hbm, panel_hbm, solved_hbm, sketch_hbm)
    inverses, coupling, panel, solved_t, sketch, sems = held
    copies = [
        pltpu.make_async_copy(source, target, sems.at[k])
        for k, (source, target) in enumerate(zip(sources, held))
    ]
    for copy in copies:
        copy.start()

    copies[0].wait()
    both = jnp.concatenate([inverses[1], inverses[0]], axis=0)
    both = permuted(both, lambda m: 32 * (m % 16 // 4) + 4 * (m // 16) + m % 4)
    both = staggered(both, 16)
    group = lax.broadcasted_iota(jnp.int32, (32, 128), 1) // 16
    row = lax.broadcasted_iota(jnp.int32, (32, 128), 0)
    for c2 in range(8):
        kept = jnp.where(group == (c2 + row) % 8, both, 0.0)
        kept = kept.reshape(4, 8, 128).sum(axis=1)
        for x2 in range(4):
            out[8 * x2 + c2, 2:6] = kept

    copies[1].wait()
    couple = permuted(
        coupling[...], lambda m: 64 * (m % 16 // 8) + 16 * (m // 32) + 8 * (m % 32 // 16) + m % 8
    )
    couple = staggered(couple, 32)
    group = group[:16] // 2
    row = row[:16]
    for x2 in range(4):
        kept = jnp.where(group == (x2 + row) % 4, couple, 0.0)
        for g in range(4):
            piece = jnp.sum(jnp.where(row // 4 == g, kept, 0.0), axis=0, keepdims=True)
            out[8 * x2 + g, 6:7] = piece
            out[8 * x2 + 4 + g, 6:7] = piece
            out[8 * x2 + g, 7:8] = piece
            out[8 * x2 + 4 + g, 7:8] = piece

    for copy in copies[2:]:
        copy.wait()
    products = lax.dot_general(
        two_parts(panel[...]), two_parts(solved_t[...]), NT, preferred_element_type=jnp.float32
    )
    total = products[:32] + products[32:]
    total = total[:, :64] + total[:, 64:]
    total = jnp.where(where[1] == 0, sketch[...], 0.0) - total
    for c2 in range(8):
        piece = packed(total[4 * c2 : 4 * c2 + 4])
        for x2 in range(4):
            out[8 * x2 + c2, 0:2] = piece


def split_body(where, got, out):
    x, c = where[0], where[1]
    right = [unpacked(got[8 * k : 8 * k + 8, 0:2].sum(axis=0)) for k in range(4)]
    right = jnp.concatenate(
        [jnp.concatenate(right[:2], axis=0), jnp.concatenate(right[2:], axis=0)], axis=1
    )
    group = lax.broadcasted_iota(jnp.int32, (8, 128), 1) // 16
    row = lax.broadcasted_iota(jnp.int32, (8, 128), 0)

    mats = [jnp.zeros((8, 128), jnp.float32) for _ in range(4)]
    for c1 in range(8):
        piece = got[8 * x + c1, 2:6]
        piece = pltpu.roll(piece, (16 * (c1 + 8) - 16 * c) % 128, 1)
        for k in range(4):
            mats[k] = jnp.where(group == (c1 + row) % 8, piece[k : k + 1], mats[k])
    mats = [staggered(mat, -16) for mat in mats]

    halves = [jnp.zeros((8, 128), jnp.float32) for _ in range(2)]
    for a in range(2):
        for c1 in range(8):
            piece = got[8 * (c // 4 + 2 * a) + c1, 6:8]
            piece = pltpu.roll(piece, (16 * c1 + 128 - 32 * x) % 128, 1)[:1]
            for h in range(2):
                here = (group == (2 * row + h + c1) % 8) & (row // 4 == a)
                halves[h] = jnp.where(here, piece, halves[h])
    halves = [staggered(half, -32, -16 * h) for h, half in enumerate(halves)]

    for k in range(8):
        for h in range(2):
            out[2 * k + h, 0:8] = right
            out[2 * k + h, 8:16] = mats[h]
            out[2 * k + h, 16:24] = halves[h]
            out[2 * k + h, 24:32] = mats[2 + h]


def last_body(got, out):
    right = unpacked(got[8:16, 0:8]).reshape(128, 64)
    terms = packed(dot(got[:, 8:16].reshape(128, 128), right))
    for k in range(8):
        out[k] = terms


def bent_body(where, parts, got, out, held):
    y_last = unpacked(parts[...].sum(axis=0))
    held[...] = y_last
    bent = dot(got[:, 16:24].reshape(128, 128), y_last).reshape(8, 2, 8, 64)
    bent = jnp.concatenate([bent[:, 0].reshape(64, 64), bent[:, 1].reshape(64, 64)], axis=1)
    piece = packed(held[pl.ds(pl.multiple_of(where[3], 32), 32), :])
    for k in range(8):
        out[k, :64] = bent
        out[k, 64:] = piece


def first_body(parts, got, out):
    bent = parts[:, :64].sum(axis=0)
    right = unpacked(got[0:8, 0:8] - bent.reshape(8, 8, 128)).reshape(128, 64)
    terms = dot(got[:, 24:32].reshape(128, 128), right)
    for g in range(4):
        piece = packed(terms[32 * g : 32 * g + 32])
        for k in range(16):
            out[4 * k + g] = piece


def design_body(where, first, last, design, out, held):
    for h in range(2):
        for x in range(4):
            k = 4 * h + x
            piece = first[8 * k : 8 * k + 8].sum(axis=0)
            piece = jnp.where(where[1] < 4, piece, last[k, 64:80])
            for z in range(4):
                row = 64 * z + 16 * x + 8 * h
                held[row : row + 8, :] = piece[
                    8 * (z % 2) : 8 * (z % 2) + 8, 64 * (z // 2) : 64 * (z // 2) + 64
                ]
    turned = held[...].T.astype(jnp.bfloat16)
    own = held[pl.ds(pl.multiple_of(where[4], 32), 32), :]
    own = jnp.concatenate([own[8 * k : 8 * k + 8] for k in range(4)], axis=1)
    for k in range(8):
        out[k, :64] = lax.dot_general(
            turned, design[256 * k : 256 * k + 256], NT, preferred_element_type=jnp.float32
        )
        out[k, 64:] = own


def leverage_body(where, got, prior_t, solution_rows, leverage):
    total = prior_t[...] + got[:, :64].sum(axis=0)
    leverage[...] = jnp.sum(total * total, axis=0, keepdims=True) * (1.0 / 64)
    own = got[where[2], 64:72]
    for k in range(4):
        solution_rows[8 * k : 8 * k + 8, :] = own[:, 64 * k : 64 * k + 64]


def local(panel, solved, sketch, inverses, coupling, design, prior):
    zh, zl, x, c = (lax.axis_index(name) for name in ("zh", "zl", "x", "c"))

    where = jnp.stack([x, c, zh, 32 * (c % 4), 32 * (4 * zl + x)])

    message = call(
        start_body,
        f32(32, 8, 128),
        where,
        panel,
        solved.T,
        sketch,
        inverses,
        coupling,
        specs=[SMEM] + [pl.BlockSpec(memory_space=pl.ANY)] * 5,
        scratch=[
            pltpu.VMEM((2, 16, 128), jnp.float32),
            pltpu.VMEM((16, 128), jnp.float32),
            pltpu.VMEM((32, 4096), jnp.float32),
            pltpu.VMEM((64, 4096), jnp.float32),
            pltpu.VMEM((32, 64), jnp.float32),
            pltpu.SemaphoreType.DMA((5,)),
        ],
        limit=56329502,
    )
    got = exchange(message, ("x", "c"))

    message = call(split_body, f32(16, 32, 128), where, got, specs=[SMEM, VMEM])
    got = exchange(message, ("zh", "zl"))

    parts = exchange(call(last_body, f32(8, 64, 128), got), "c")

    last = exchange(
        call(
            bent_body,
            f32(8, 80, 128),
            where,
            parts,
            got,
            specs=[SMEM, VMEM, VMEM],
            scratch=[pltpu.VMEM((128, 64), jnp.float32)],
        ),
        ("zl", "x"),
    )

    first = exchange(call(first_body, f32(64, 16, 128), last, got), ("zl", "x", "c"))

    message = call(
        design_body,
        f32(8, 72, 256),
        where,
        first,
        last,
        design,
        specs=[SMEM, VMEM, VMEM, VMEM],
        scratch=[pltpu.VMEM((256, 64), jnp.float32)],
    )
    got = exchange(message, "c")
    block_solution, leverage = call(
        leverage_body,
        (f32(32, 64), f32(1, 256)),
        where,
        got,
        prior.T,
        specs=[SMEM, VMEM, VMEM],
    )
    return block_solution, leverage.reshape(256)


def solution(mesh):
    fine = Mesh(mesh.devices.reshape(8, 2, 4, 8), ("zh", "zl", "x", "c"))
    r = ("zh", "zl", "x")
    in_specs = (
        P(r, "c"),
        P("c", None),
        P(r, None),
        P(None, r, "c"),
        P(r, "c"),
        P(r, "c"),
        P((*r, "c"), None),
    )
    out_specs = (P(r, None), P((*r, "c")))
    return jax.shard_map(local, mesh=fine, in_specs=in_specs, out_specs=out_specs, check_vma=False)
```

```python
import jax
import jax.numpy as jnp
from jax import lax
from jax.experimental import pallas as pl
from jax.experimental.pallas import tpu as pltpu
from jax.sharding import Mesh
from jax.sharding import PartitionSpec as P

HIGHEST = lax.Precision.HIGHEST
VMEM = pl.BlockSpec(memory_space=pltpu.VMEM)
NT = (((1,), (1,)), ((), ()))


def dot(a, b):
    return jnp.dot(a, b, precision=HIGHEST, preferred_element_type=jnp.float32)


def exchange(value, axes):
    return lax.all_to_all(value, axes, 0, 0, tiled=True)


def packed(value):
    half = value.shape[-2] // 2
    return jnp.concatenate([value[..., :half, :], value[..., half:, :]], axis=-1)


def unpacked(value):
    return jnp.concatenate([value[..., :64], value[..., 64:]], axis=-2)


def call(body, out, *args, specs=None, scratch=(), limit=32 << 20):
    return pl.pallas_call(
        body,
        out_shape=out,
        in_specs=specs or [VMEM] * len(args),
        out_specs=jax.tree.map(lambda _: VMEM, out),
        scratch_shapes=scratch,
        compiler_params=pltpu.CompilerParams(vmem_limit_bytes=limit),
    )(*args)


def f32(*shape):
    return jax.ShapeDtypeStruct(shape, jnp.float32)


def two_parts(value):
    high = value.astype(jnp.bfloat16)
    low = (value - high.astype(jnp.float32)).astype(jnp.bfloat16)
    return jnp.concatenate([high, low], axis=0)


def permuted(value, source_of):
    row = lax.broadcasted_iota(jnp.int32, (128, 128), 0)
    lane = lax.broadcasted_iota(jnp.int32, (128, 128), 1)
    return dot(value, (row == source_of(lane)).astype(jnp.float32))


def staggered(value, step, shift=0):
    row = lax.broadcasted_iota(jnp.int32, value.shape, 0) % (128 // (step % 128 & -(step % 128)))
    out = value
    for i in range(128 // (step % 128 & -(step % 128))):
        turn = (shift + step * i) % 128
        out = jnp.where(row == i, pltpu.roll(value, turn, 1) if turn else value, out)
    return out


def start_body(panel_hbm, solved_hbm, sketch_hbm, inverses_hbm, coupling_hbm, out, *held):
    sources = (inverses_hbm, coupling_hbm, panel_hbm, solved_hbm, sketch_hbm)
    inverses, coupling, panel, solved_t, sketch, sems = held
    copies = [
        pltpu.make_async_copy(source, target, sems.at[k])
        for k, (source, target) in enumerate(zip(sources, held))
    ]
    for copy in copies:
        copy.start()

    copies[0].wait()
    both = jnp.concatenate([inverses[1], inverses[0]], axis=0)
    both = permuted(both, lambda m: 32 * (m % 16 // 4) + 4 * (m // 16) + m % 4)
    both = staggered(both, 16)
    group = lax.broadcasted_iota(jnp.int32, (32, 128), 1) // 16
    row = lax.broadcasted_iota(jnp.int32, (32, 128), 0)
    for c2 in range(8):
        kept = jnp.where(group == (c2 + row) % 8, both, 0.0)
        kept = kept.reshape(4, 8, 128).sum(axis=1)
        for x2 in range(4):
            out[8 * x2 + c2, 2:6] = kept

    copies[1].wait()
    couple = permuted(
        coupling[...], lambda m: 64 * (m % 16 // 8) + 16 * (m // 32) + 8 * (m % 32 // 16) + m % 8
    )
    couple = staggered(couple, 32)
    group = group[:16] // 2
    row = row[:16]
    for x2 in range(4):
        kept = jnp.where(group == (x2 + row) % 4, couple, 0.0)
        for g in range(4):
            piece = jnp.sum(jnp.where(row // 4 == g, kept, 0.0), axis=0, keepdims=True)
            out[8 * x2 + g, 6:7] = piece
            out[8 * x2 + 4 + g, 6:7] = piece
            out[8 * x2 + g, 7:8] = piece
            out[8 * x2 + 4 + g, 7:8] = piece

    for copy in copies[2:]:
        copy.wait()
    products = lax.dot_general(
        two_parts(panel[...]), two_parts(solved_t[...]), NT, preferred_element_type=jnp.float32
    )
    total = products[:32] + products[32:]
    total = total[:, :64] + total[:, 64:]
    total = jnp.where(lax.axis_index("c") == 0, sketch[...], 0.0) - total
    for c2 in range(8):
        piece = packed(total[4 * c2 : 4 * c2 + 4])
        for x2 in range(4):
            out[8 * x2 + c2, 0:2] = piece


def split_body(got, out):
    x, c = lax.axis_index("x"), lax.axis_index("c")
    right = [unpacked(got[8 * k : 8 * k + 8, 0:2].sum(axis=0)) for k in range(4)]
    right = jnp.concatenate(
        [jnp.concatenate(right[:2], axis=0), jnp.concatenate(right[2:], axis=0)], axis=1
    )
    group = lax.broadcasted_iota(jnp.int32, (8, 128), 1) // 16
    row = lax.broadcasted_iota(jnp.int32, (8, 128), 0)

    mats = [jnp.zeros((8, 128), jnp.float32) for _ in range(4)]
    for c1 in range(8):
        piece = got[8 * x + c1, 2:6]
        piece = pltpu.roll(piece, (16 * (c1 + 8) - 16 * c) % 128, 1)
        for k in range(4):
            mats[k] = jnp.where(group == (c1 + row) % 8, piece[k : k + 1], mats[k])
    mats = [staggered(mat, -16) for mat in mats]

    halves = [jnp.zeros((8, 128), jnp.float32) for _ in range(2)]
    for a in range(2):
        for c1 in range(8):
            piece = got[8 * (c // 4 + 2 * a) + c1, 6:8]
            piece = pltpu.roll(piece, (16 * c1 + 128 - 32 * x) % 128, 1)[:1]
            for h in range(2):
                here = (group == (2 * row + h + c1) % 8) & (row // 4 == a)
                halves[h] = jnp.where(here, piece, halves[h])
    halves = [staggered(half, -32, -16 * h) for h, half in enumerate(halves)]

    for k in range(8):
        for h in range(2):
            out[2 * k + h, 0:8] = right
            out[2 * k + h, 8:16] = mats[h]
            out[2 * k + h, 16:24] = halves[h]
            out[2 * k + h, 24:32] = mats[2 + h]


def last_body(got, out):
    right = unpacked(got[8:16, 0:8]).reshape(128, 64)
    terms = packed(dot(got[:, 8:16].reshape(128, 128), right))
    for k in range(8):
        out[k] = terms


def bent_body(parts, got, out, y_out):
    y_last = unpacked(parts[...].sum(axis=0))
    bent = dot(got[:, 16:24].reshape(128, 128), y_last).reshape(8, 2, 8, 64)
    bent = jnp.concatenate([bent[:, 0].reshape(64, 64), bent[:, 1].reshape(64, 64)], axis=1)
    for k in range(8):
        out[k] = bent
    for g in range(4):
        y_out[g] = packed(y_last[32 * g : 32 * g + 32])


def first_body(parts, y_last, got, out):
    bent = parts[...].sum(axis=0)
    right = unpacked(got[0:8, 0:8] - bent.reshape(8, 8, 128)).reshape(128, 64)
    terms = dot(got[:, 24:32].reshape(128, 128), right)
    for g in range(4):
        piece = packed(terms[32 * g : 32 * g + 32])
        last = y_last[g]
        for k in range(8):
            out[8 * k + g] = piece
            out[8 * k + 4 + g] = last


def design_body(parts, design, out, held):
    c = lax.axis_index("c")
    for h in range(2):
        for x in range(4):
            k = 4 * h + x
            piece = parts[8 * k : 8 * k + 8].sum(axis=0)
            piece = jnp.where(c < 4, piece, parts[8 * k])
            for z in range(4):
                row = 64 * z + 16 * x + 8 * h
                held[row : row + 8, :] = piece[
                    8 * (z % 2) : 8 * (z % 2) + 8, 64 * (z // 2) : 64 * (z // 2) + 64
                ]
    turned = held[...].T.astype(jnp.bfloat16)
    own = 32 * (4 * lax.axis_index("zl") + lax.axis_index("x"))
    own = held[pl.ds(pl.multiple_of(own, 32), 32), :]
    own = jnp.concatenate([own[8 * k : 8 * k + 8] for k in range(4)], axis=1)
    for k in range(8):
        out[k, :64] = lax.dot_general(
            turned, design[256 * k : 256 * k + 256], NT, preferred_element_type=jnp.float32
        )
        out[k, 64:] = own


def leverage_body(got, prior_t, solution_rows, leverage):
    total = prior_t[...] + got[:, :64].sum(axis=0)
    leverage[...] = jnp.sum(total * total, axis=0, keepdims=True) * (1.0 / 64)
    own = got[lax.axis_index("zh"), 64:72]
    for k in range(4):
        solution_rows[8 * k : 8 * k + 8, :] = own[:, 64 * k : 64 * k + 64]


def local(panel, solved, sketch, inverses, coupling, design, prior):
    message = call(
        start_body,
        f32(32, 8, 128),
        panel,
        solved.T,
        sketch,
        inverses,
        coupling,
        specs=[pl.BlockSpec(memory_space=pl.ANY)] * 5,
        scratch=[
            pltpu.VMEM((2, 16, 128), jnp.float32),
            pltpu.VMEM((16, 128), jnp.float32),
            pltpu.VMEM((32, 4096), jnp.float32),
            pltpu.VMEM((64, 4096), jnp.float32),
            pltpu.VMEM((32, 64), jnp.float32),
            pltpu.SemaphoreType.DMA((5,)),
        ],
        limit=60 << 20,
    )
    got = exchange(message, ("x", "c"))

    got = exchange(call(split_body, f32(16, 32, 128), got), ("zh", "zl"))

    parts = exchange(call(last_body, f32(8, 64, 128), got), "c")

    bent, y_last = call(bent_body, (f32(8, 64, 128), f32(4, 16, 128)), parts, got)
    parts = exchange(bent, ("zl", "x"))

    parts = exchange(call(first_body, f32(64, 16, 128), parts, y_last, got), ("zl", "x", "c"))

    message = call(
        design_body, f32(8, 72, 256), parts, design, scratch=[pltpu.VMEM((256, 64), jnp.float32)]
    )
    got = exchange(message, "c")
    block_solution, leverage = call(leverage_body, (f32(32, 64), f32(1, 256)), got, prior.T)
    return block_solution, leverage.reshape(256)


def solution(mesh):
    fine = Mesh(mesh.devices.reshape(8, 2, 4, 8), ("zh", "zl", "x", "c"))
    r = ("zh", "zl", "x")
    in_specs = (
        P(r, "c"),
        P("c", None),
        P(r, None),
        P(None, r, "c"),
        P(r, "c"),
        P(r, "c"),
        P((*r, "c"), None),
    )
    out_specs = (P(r, None), P((*r, "c")))
    return jax.shard_map(local, mesh=fine, in_specs=in_specs, out_specs=out_specs, check_vma=False)
```

```python
import jax
import jax.numpy as jnp
from jax import lax
from jax.experimental import pallas as pl
from jax.experimental.pallas import tpu as pltpu
from jax.sharding import Mesh
from jax.sharding import PartitionSpec as P

HIGHEST = lax.Precision.HIGHEST
VMEM = pl.BlockSpec(memory_space=pltpu.VMEM)
NT = (((1,), (1,)), ((), ()))
CHUNKS = 4


def dot(a, b):
    return jnp.dot(a, b, precision=HIGHEST, preferred_element_type=jnp.float32)


def exchange(value, axes):
    return lax.all_to_all(value, axes, 0, 0, tiled=True)


def packed(value):
    half = value.shape[-2] // 2
    return jnp.concatenate([value[..., :half, :], value[..., half:, :]], axis=-1)


def unpacked(value):
    return jnp.concatenate([value[..., :64], value[..., 64:]], axis=-2)


def call(body, out, *args, specs=None, scratch=(), limit=32 << 20):
    return pl.pallas_call(
        body,
        out_shape=out,
        in_specs=specs or [VMEM] * len(args),
        out_specs=jax.tree.map(lambda _: VMEM, out),
        scratch_shapes=scratch,
        compiler_params=pltpu.CompilerParams(vmem_limit_bytes=limit),
    )(*args)


def f32(*shape):
    return jax.ShapeDtypeStruct(shape, jnp.float32)


def two_parts(value):
    high = value.astype(jnp.bfloat16)
    low = (value - high.astype(jnp.float32)).astype(jnp.bfloat16)
    return jnp.concatenate([high, low], axis=0)


def permuted(value, source_of):
    row = lax.broadcasted_iota(jnp.int32, (128, 128), 0)
    lane = lax.broadcasted_iota(jnp.int32, (128, 128), 1)
    return dot(value, (row == source_of(lane)).astype(jnp.float32))


def staggered(value, step, shift=0):
    row = lax.broadcasted_iota(jnp.int32, value.shape, 0) % (128 // (step % 128 & -(step % 128)))
    out = value
    for i in range(128 // (step % 128 & -(step % 128))):
        turn = (shift + step * i) % 128
        out = jnp.where(row == i, pltpu.roll(value, turn, 1) if turn else value, out)
    return out


def start_body(panel_hbm, solved_hbm, sketch_hbm, inverses_hbm, coupling_hbm, out, *held):
    inverses, coupling, sketch, panel, solved_t, sems = held
    pairs = [(inverses_hbm, inverses), (coupling_hbm, coupling), (sketch_hbm, sketch)]
    for k in range(CHUNKS):
        span = pl.ds(k * (4096 // CHUNKS), 4096 // CHUNKS)
        pairs += [(solved_hbm.at[:, span], solved_t.at[k]), (panel_hbm.at[:, span], panel.at[k])]
    copies = [
        pltpu.make_async_copy(source, target, sems.at[k])
        for k, (source, target) in enumerate(pairs)
    ]
    for copy in copies:
        copy.start()

    copies[0].wait()
    both = jnp.concatenate([inverses[1], inverses[0]], axis=0)
    both = permuted(both, lambda m: 32 * (m % 16 // 4) + 4 * (m // 16) + m % 4)
    both = staggered(both, 16)
    group = lax.broadcasted_iota(jnp.int32, (32, 128), 1) // 16
    row = lax.broadcasted_iota(jnp.int32, (32, 128), 0)
    for c2 in range(8):
        kept = jnp.where(group == (c2 + row) % 8, both, 0.0)
        kept = kept.reshape(4, 8, 128).sum(axis=1)
        for x2 in range(4):
            out[8 * x2 + c2, 2:6] = kept

    copies[1].wait()
    couple = permuted(
        coupling[...], lambda m: 64 * (m % 16 // 8) + 16 * (m // 32) + 8 * (m % 32 // 16) + m % 8
    )
    couple = staggered(couple, 32)
    group = group[:16] // 2
    row = row[:16]
    for x2 in range(4):
        kept = jnp.where(group == (x2 + row) % 4, couple, 0.0)
        for g in range(4):
            piece = jnp.sum(jnp.where(row // 4 == g, kept, 0.0), axis=0, keepdims=True)
            out[8 * x2 + g, 6:7] = piece
            out[8 * x2 + 4 + g, 6:7] = piece
            out[8 * x2 + g, 7:8] = piece
            out[8 * x2 + 4 + g, 7:8] = piece

    copies[2].wait()
    products = jnp.zeros((64, 128), jnp.float32)
    for k in range(CHUNKS):
        copies[3 + 2 * k].wait()
        copies[4 + 2 * k].wait()
        products += lax.dot_general(
            two_parts(panel[k]), two_parts(solved_t[k]), NT, preferred_element_type=jnp.float32
        )
    total = products[:32] + products[32:]
    total = total[:, :64] + total[:, 64:]
    total = jnp.where(lax.axis_index("c") == 0, sketch[...], 0.0) - total
    for c2 in range(8):
        piece = packed(total[4 * c2 : 4 * c2 + 4])
        for x2 in range(4):
            out[8 * x2 + c2, 0:2] = piece


def split_body(got, out):
    x, c = lax.axis_index("x"), lax.axis_index("c")
    right = [unpacked(got[8 * k : 8 * k + 8, 0:2].sum(axis=0)) for k in range(4)]
    right = jnp.concatenate(
        [jnp.concatenate(right[:2], axis=0), jnp.concatenate(right[2:], axis=0)], axis=1
    )
    group = lax.broadcasted_iota(jnp.int32, (8, 128), 1) // 16
    row = lax.broadcasted_iota(jnp.int32, (8, 128), 0)

    mats = [jnp.zeros((8, 128), jnp.float32) for _ in range(4)]
    for c1 in range(8):
        piece = got[8 * x + c1, 2:6]
        piece = pltpu.roll(piece, (16 * (c1 + 8) - 16 * c) % 128, 1)
        for k in range(4):
            mats[k] = jnp.where(group == (c1 + row) % 8, piece[k : k + 1], mats[k])
    mats = [staggered(mat, -16) for mat in mats]

    halves = [jnp.zeros((8, 128), jnp.float32) for _ in range(2)]
    for a in range(2):
        for c1 in range(8):
            piece = got[8 * (c // 4 + 2 * a) + c1, 6:8]
            piece = pltpu.roll(piece, (16 * c1 + 128 - 32 * x) % 128, 1)[:1]
            for h in range(2):
                here = (group == (2 * row + h + c1) % 8) & (row // 4 == a)
                halves[h] = jnp.where(here, piece, halves[h])
    halves = [staggered(half, -32, -16 * h) for h, half in enumerate(halves)]

    own = got[pl.ds(pl.multiple_of(8 * x, 8), 8), 0:2].sum(axis=0)
    for h in range(2):
        near = jnp.concatenate([mats[h][:, :64], mats[2 + h][:, :64]], axis=1)
        far = jnp.concatenate([mats[h][:, 64:], mats[2 + h][:, 64:]], axis=1)
        near = jnp.where(lax.axis_index("zh") < 4, near, right)
        piece = own[:, 64 * h : 64 * h + 64]
        piece = jnp.concatenate([piece[0:1], piece[1:2]], axis=1)
        piece = jnp.concatenate([piece, piece], axis=0)
        for k in range(8):
            for m, tile in enumerate((near, far, halves[h])):
                for j in range(4):
                    out[2 * k + h, 4 * m + j] = tile[2 * j : 2 * j + 2]
            out[2 * k + h, 12] = piece


def applied(got, lanes, vector):
    terms = dot(got[:, 8:16, lanes].reshape(128, 64), vector[64:])
    near = dot(got[0:8, 0:8, lanes].reshape(64, 64), vector[:64])
    return jnp.concatenate([terms[:64] + near, terms[64:]], axis=0)


def last_body(got, out):
    right = unpacked(got[8:16, 0:8]).reshape(128, 64)
    terms = packed(applied(got, slice(0, 64), right))
    for k in range(8):
        out[k] = terms


def bent_body(parts, got, out, y_out):
    y_last = unpacked(parts[...].sum(axis=0))
    bent = dot(got[:, 16:24].reshape(128, 128), y_last).reshape(8, 2, 8, 64)
    bent = jnp.concatenate([bent[:, 0].reshape(64, 64), bent[:, 1].reshape(64, 64)], axis=1)

    x, h = lax.axis_index("x"), lax.axis_index("zl")
    row = lax.broadcasted_iota(jnp.int32, (8, 128), 0)
    half = lax.broadcasted_iota(jnp.int32, (8, 128), 1) // 64
    here = (half == x // 2) & (row // 2 == 2 * (x % 2) + h)
    rows = []
    for z in range(8):
        piece = got[z, 24:25]
        piece = jnp.where(row % 2 == x // 2, piece, pltpu.roll(piece, 64, 1))
        rows.append(jnp.where(here, piece, 0.0))
    terms = jnp.concatenate(rows, axis=0) - bent
    for k in range(8):
        out[k] = terms
    for g in range(4):
        y_out[g] = packed(y_last[32 * g : 32 * g + 32])


def first_body(parts, y_last, got, out):
    right = unpacked(parts[...].sum(axis=0).reshape(8, 8, 128)).reshape(128, 64)
    terms = applied(got, slice(64, 128), right)
    for g in range(4):
        piece = packed(terms[32 * g : 32 * g + 32])
        last = y_last[g]
        for k in range(8):
            out[8 * k + g] = piece
            out[8 * k + 4 + g] = last


def design_body(parts, design, out, held):
    c = lax.axis_index("c")
    for h in range(2):
        for x in range(4):
            k = 4 * h + x
            piece = parts[8 * k : 8 * k + 8].sum(axis=0)
            piece = jnp.where(c < 4, piece, parts[8 * k])
            for z in range(4):
                row = 64 * z + 16 * x + 8 * h
                held[row : row + 8, :] = piece[
                    8 * (z % 2) : 8 * (z % 2) + 8, 64 * (z // 2) : 64 * (z // 2) + 64
                ]
    turned = held[...].T.astype(jnp.bfloat16)
    own = 32 * (4 * lax.axis_index("zl") + lax.axis_index("x"))
    own = held[pl.ds(pl.multiple_of(own, 32), 32), :]
    own = jnp.concatenate([own[8 * k : 8 * k + 8] for k in range(4)], axis=1)
    for k in range(8):
        out[k, :64] = lax.dot_general(
            turned, design[256 * k : 256 * k + 256], NT, preferred_element_type=jnp.float32
        )
        out[k, 64:] = own


def leverage_body(got, prior_t, solution_rows, leverage):
    total = prior_t[...] + got[:, :64].sum(axis=0)
    leverage[...] = jnp.sum(total * total, axis=0, keepdims=True) * (1.0 / 64)
    own = got[lax.axis_index("zh"), 64:72]
    for k in range(4):
        solution_rows[8 * k : 8 * k + 8, :] = own[:, 64 * k : 64 * k + 64]


def local(panel, solved, sketch, inverses, coupling, design, prior):
    message = call(
        start_body,
        f32(32, 8, 128),
        *(
            pltpu.with_memory_space_constraint(value, pltpu.HBM)
            for value in (panel, solved.T, sketch, inverses, coupling)
        ),
        specs=[pl.BlockSpec(memory_space=pl.ANY)] * 5,
        scratch=[
            pltpu.VMEM((2, 16, 128), jnp.float32),
            pltpu.VMEM((16, 128), jnp.float32),
            pltpu.VMEM((32, 64), jnp.float32),
            pltpu.VMEM((CHUNKS, 32, 4096 // CHUNKS), jnp.float32),
            pltpu.VMEM((CHUNKS, 64, 4096 // CHUNKS), jnp.float32),
            pltpu.SemaphoreType.DMA((3 + 2 * CHUNKS,)),
        ],
    )
    got = exchange(message, ("x", "c"))

    got = exchange(call(split_body, f32(16, 13, 2, 128), got), ("zh", "zl")).reshape(16, 26, 128)

    parts = exchange(call(last_body, f32(8, 64, 128), got), "c")

    bent, y_last = call(bent_body, (f32(8, 64, 128), f32(4, 16, 128)), parts, got)
    parts = exchange(bent, ("zl", "x"))

    parts = exchange(call(first_body, f32(64, 16, 128), parts, y_last, got), ("zl", "x", "c"))

    message = call(
        design_body, f32(8, 72, 256), parts, design, scratch=[pltpu.VMEM((256, 64), jnp.float32)]
    )
    got = exchange(message, "c")
    block_solution, leverage = call(leverage_body, (f32(32, 64), f32(1, 256)), got, prior.T)
    return block_solution, leverage.reshape(256)


def solution(mesh):
    fine = Mesh(mesh.devices.reshape(8, 2, 4, 8), ("zh", "zl", "x", "c"))
    r = ("zh", "zl", "x")
    in_specs = (
        P(r, "c"),
        P("c", None),
        P(r, None),
        P(None, r, "c"),
        P(r, "c"),
        P(r, "c"),
        P((*r, "c"), None),
    )
    out_specs = (P(r, None), P((*r, "c")))
    return jax.shard_map(local, mesh=fine, in_specs=in_specs, out_specs=out_specs, check_vma=False)
```

```python
import jax
import jax.numpy as jnp
from jax import lax
from jax.experimental import pallas as pl
from jax.experimental.pallas import tpu as pltpu
from jax.sharding import Mesh
from jax.sharding import PartitionSpec as P

HIGHEST = lax.Precision.HIGHEST
VMEM = pl.BlockSpec(memory_space=pltpu.VMEM)
NT = (((1,), (1,)), ((), ()))
CHUNKS = 4


def dot(a, b):
    return jnp.dot(a, b, precision=HIGHEST, preferred_element_type=jnp.float32)


def exchange(value, axes):
    return lax.all_to_all(value, axes, 0, 0, tiled=True)


def packed(value):
    half = value.shape[-2] // 2
    return jnp.concatenate([value[..., :half, :], value[..., half:, :]], axis=-1)


def unpacked(value):
    return jnp.concatenate([value[..., :64], value[..., 64:]], axis=-2)


def call(body, out, *args, specs=None, scratch=(), limit=32 << 20):
    return pl.pallas_call(
        body,
        out_shape=out,
        in_specs=specs or [VMEM] * len(args),
        out_specs=jax.tree.map(lambda _: VMEM, out),
        scratch_shapes=scratch,
        compiler_params=pltpu.CompilerParams(vmem_limit_bytes=limit),
    )(*args)


def f32(*shape):
    return jax.ShapeDtypeStruct(shape, jnp.float32)


def two_parts(value):
    high = value.astype(jnp.bfloat16)
    low = (value - high.astype(jnp.float32)).astype(jnp.bfloat16)
    return jnp.concatenate([high, low], axis=0)


def permuted(value, source_of):
    row = lax.broadcasted_iota(jnp.int32, (128, 128), 0)
    lane = lax.broadcasted_iota(jnp.int32, (128, 128), 1)
    return dot(value, (row == source_of(lane)).astype(jnp.float32))


def staggered(value, step, shift=0):
    row = lax.broadcasted_iota(jnp.int32, value.shape, 0) % (128 // (step % 128 & -(step % 128)))
    out = value
    for i in range(128 // (step % 128 & -(step % 128))):
        turn = (shift + step * i) % 128
        out = jnp.where(row == i, pltpu.roll(value, turn, 1) if turn else value, out)
    return out


def start_body(panel_hbm, solved_hbm, sketch_hbm, inverses_hbm, coupling_hbm, out, *held):
    inverses, coupling, sketch, panel, solved_t, sems = held
    pairs = [(inverses_hbm, inverses), (coupling_hbm, coupling), (sketch_hbm, sketch)]
    for k in range(CHUNKS):
        span = pl.ds(k * (4096 // CHUNKS), 4096 // CHUNKS)
        pairs += [(solved_hbm.at[:, span], solved_t.at[k]), (panel_hbm.at[:, span], panel.at[k])]
    copies = [
        pltpu.make_async_copy(source, target, sems.at[k])
        for k, (source, target) in enumerate(pairs)
    ]
    for copy in copies:
        copy.start()

    copies[0].wait()
    both = jnp.concatenate([inverses[1], inverses[0]], axis=0)
    both = permuted(both, lambda m: 32 * (m % 16 // 4) + 4 * (m // 16) + m % 4)
    both = staggered(both, 16)
    group = lax.broadcasted_iota(jnp.int32, (32, 128), 1) // 16
    row = lax.broadcasted_iota(jnp.int32, (32, 128), 0)
    for c2 in range(8):
        kept = jnp.where(group == (c2 + row) % 8, both, 0.0)
        kept = kept.reshape(4, 8, 128).sum(axis=1)
        for x2 in range(4):
            out[8 * x2 + c2, 2:6] = kept

    copies[1].wait()
    couple = permuted(
        coupling[...], lambda m: 64 * (m % 16 // 8) + 16 * (m // 32) + 8 * (m % 32 // 16) + m % 8
    )
    couple = staggered(couple, 32)
    group = group[:16] // 2
    row = row[:16]
    for x2 in range(4):
        kept = jnp.where(group == (x2 + row) % 4, couple, 0.0)
        for g in range(4):
            piece = jnp.sum(jnp.where(row // 4 == g, kept, 0.0), axis=0, keepdims=True)
            out[8 * x2 + g, 6:7] = piece
            out[8 * x2 + 4 + g, 6:7] = piece
            out[8 * x2 + g, 7:8] = piece
            out[8 * x2 + 4 + g, 7:8] = piece

    copies[2].wait()
    products = jnp.zeros((64, 128), jnp.float32)
    for k in range(CHUNKS):
        copies[3 + 2 * k].wait()
        copies[4 + 2 * k].wait()
        products += lax.dot_general(
            two_parts(panel[k]), two_parts(solved_t[k]), NT, preferred_element_type=jnp.float32
        )
    total = products[:32] + products[32:]
    total = total[:, :64] + total[:, 64:]
    total = jnp.where(lax.axis_index("c") == 0, sketch[...], 0.0) - total
    for c2 in range(8):
        piece = packed(total[4 * c2 : 4 * c2 + 4])
        for x2 in range(4):
            out[8 * x2 + c2, 0:2] = piece


def split_body(got, out):
    x, c = lax.axis_index("x"), lax.axis_index("c")
    right = [unpacked(got[8 * k : 8 * k + 8, 0:2].sum(axis=0)) for k in range(4)]
    right = jnp.concatenate(
        [jnp.concatenate(right[:2], axis=0), jnp.concatenate(right[2:], axis=0)], axis=1
    )
    group = lax.broadcasted_iota(jnp.int32, (8, 128), 1) // 16
    row = lax.broadcasted_iota(jnp.int32, (8, 128), 0)

    mats = [jnp.zeros((8, 128), jnp.float32) for _ in range(4)]
    for c1 in range(8):
        piece = got[8 * x + c1, 2:6]
        piece = pltpu.roll(piece, (16 * (c1 + 8) - 16 * c) % 128, 1)
        for k in range(4):
            mats[k] = jnp.where(group == (c1 + row) % 8, piece[k : k + 1], mats[k])
    mats = [staggered(mat, -16) for mat in mats]

    halves = [jnp.zeros((8, 128), jnp.float32) for _ in range(2)]
    for a in range(2):
        for c1 in range(8):
            piece = got[8 * (c // 4 + 2 * a) + c1, 6:8]
            piece = pltpu.roll(piece, (16 * c1 + 128 - 32 * x) % 128, 1)[:1]
            for h in range(2):
                here = (group == (2 * row + h + c1) % 8) & (row // 4 == a)
                halves[h] = jnp.where(here, piece, halves[h])
    halves = [staggered(half, -32, -16 * h) for h, half in enumerate(halves)]

    own = got[pl.ds(pl.multiple_of(8 * x, 8), 8), 0:2].sum(axis=0)
    for h in range(2):
        near = jnp.concatenate([mats[h][:, :64], mats[2 + h][:, :64]], axis=1)
        far = jnp.concatenate([mats[h][:, 64:], mats[2 + h][:, 64:]], axis=1)
        near = jnp.where(lax.axis_index("zh") < 4, near, right)
        piece = own[:, 64 * h : 64 * h + 64]
        piece = jnp.concatenate([piece[0:1], piece[1:2]], axis=1)
        piece = jnp.concatenate([piece, piece], axis=0)
        for k in range(8):
            for m, tile in enumerate((near, far, halves[h])):
                for j in range(4):
                    out[2 * k + h, 4 * m + j] = tile[2 * j : 2 * j + 2]
            out[2 * k + h, 12] = piece


def applied(got, lanes, vector):
    terms = dot(got[:, 8:16, lanes].reshape(128, 64), vector[64:])
    near = dot(got[0:8, 0:8, lanes].reshape(64, 64), vector[:64])
    return jnp.concatenate([terms[:64] + near, terms[64:]], axis=0)


def last_body(got, out):
    right = unpacked(got[8:16, 0:8]).reshape(128, 64)
    terms = packed(applied(got, slice(0, 64), right))
    for k in range(8):
        out[k] = terms


def bent_body(parts, got, out, y_out):
    y_last = unpacked(parts[...].sum(axis=0))
    bent = dot(got[:, 16:24].reshape(128, 128), y_last).reshape(8, 2, 8, 64)
    bent = jnp.concatenate([bent[:, 0].reshape(64, 64), bent[:, 1].reshape(64, 64)], axis=1)

    x, h = lax.axis_index("x"), lax.axis_index("zl")
    row = lax.broadcasted_iota(jnp.int32, (8, 128), 0)
    half = lax.broadcasted_iota(jnp.int32, (8, 128), 1) // 64
    here = (half == x // 2) & (row // 2 == 2 * (x % 2) + h)
    rows = []
    for z in range(8):
        piece = got[z, 24:25]
        piece = jnp.where(row % 2 == x // 2, piece, pltpu.roll(piece, 64, 1))
        rows.append(jnp.where(here, piece, 0.0))
    terms = jnp.concatenate(rows, axis=0) - bent
    for k in range(8):
        out[k] = terms
    for g in range(4):
        y_out[g] = packed(y_last[32 * g : 32 * g + 32])


def first_body(parts, got, out):
    right = unpacked(parts[...].sum(axis=0).reshape(8, 8, 128)).reshape(128, 64)
    terms = applied(got, slice(64, 128), right)
    for g in range(4):
        piece = packed(terms[32 * g : 32 * g + 32])
        out[g] = piece
        out[4 + g] = piece


def own_body(parts, y_last, out):
    c = lax.axis_index("c")
    piece = jnp.where(c < 4, parts[...].sum(axis=0), y_last[c % 4])
    for k in range(8):
        out[k] = piece


def design_body(parts, design, out, held):
    for h in range(2):
        for x in range(4):
            piece = parts[4 * h + x]
            for z in range(4):
                row = 64 * z + 16 * x + 8 * h
                held[row : row + 8, :] = piece[
                    8 * (z % 2) : 8 * (z % 2) + 8, 64 * (z // 2) : 64 * (z // 2) + 64
                ]
    turned = held[...].T.astype(jnp.bfloat16)
    own = 32 * (4 * lax.axis_index("zl") + lax.axis_index("x"))
    own = held[pl.ds(pl.multiple_of(own, 32), 32), :]
    own = jnp.concatenate([own[8 * k : 8 * k + 8] for k in range(4)], axis=1)
    for k in range(8):
        out[k, :64] = lax.dot_general(
            turned, design[256 * k : 256 * k + 256], NT, preferred_element_type=jnp.float32
        )
        out[k, 64:] = own


def leverage_body(got, prior_t, solution_rows, leverage):
    total = prior_t[...] + got[:, :64].sum(axis=0)
    leverage[...] = jnp.sum(total * total, axis=0, keepdims=True) * (1.0 / 64)
    own = got[lax.axis_index("zh"), 64:72]
    for k in range(4):
        solution_rows[8 * k : 8 * k + 8, :] = own[:, 64 * k : 64 * k + 64]


def local(panel, solved, sketch, inverses, coupling, design, prior):
    message = call(
        start_body,
        f32(32, 8, 128),
        *(
            pltpu.with_memory_space_constraint(value, pltpu.HBM)
            for value in (panel, solved.T, sketch, inverses, coupling)
        ),
        specs=[pl.BlockSpec(memory_space=pl.ANY)] * 5,
        scratch=[
            pltpu.VMEM((2, 16, 128), jnp.float32),
            pltpu.VMEM((16, 128), jnp.float32),
            pltpu.VMEM((32, 64), jnp.float32),
            pltpu.VMEM((CHUNKS, 32, 4096 // CHUNKS), jnp.float32),
            pltpu.VMEM((CHUNKS, 64, 4096 // CHUNKS), jnp.float32),
            pltpu.SemaphoreType.DMA((3 + 2 * CHUNKS,)),
        ],
    )
    got = exchange(message, ("x", "c"))

    got = exchange(call(split_body, f32(16, 13, 2, 128), got), ("zh", "zl")).reshape(16, 26, 128)

    parts = exchange(call(last_body, f32(8, 64, 128), got), "c")

    bent, y_last = call(bent_body, (f32(8, 64, 128), f32(4, 16, 128)), parts, got)
    parts = exchange(bent, ("zl", "x"))

    parts = exchange(call(first_body, f32(8, 16, 128), parts, got), "c")
    parts = exchange(call(own_body, f32(8, 16, 128), parts, y_last), ("zl", "x"))

    message = call(
        design_body, f32(8, 72, 256), parts, design, scratch=[pltpu.VMEM((256, 64), jnp.float32)]
    )
    got = exchange(message, "c")
    block_solution, leverage = call(leverage_body, (f32(32, 64), f32(1, 256)), got, prior.T)
    return block_solution, leverage.reshape(256)


def solution(mesh):
    fine = Mesh(mesh.devices.reshape(8, 2, 4, 8), ("zh", "zl", "x", "c"))
    r = ("zh", "zl", "x")
    in_specs = (
        P(r, "c"),
        P("c", None),
        P(r, None),
        P(None, r, "c"),
        P(r, "c"),
        P(r, "c"),
        P((*r, "c"), None),
    )
    out_specs = (P(r, None), P((*r, "c")))
    return jax.shard_map(local, mesh=fine, in_specs=in_specs, out_specs=out_specs, check_vma=False)
```

```python
import jax
import jax.numpy as jnp
from jax import lax
from jax.experimental import pallas as pl
from jax.experimental.pallas import tpu as pltpu
from jax.sharding import Mesh
from jax.sharding import PartitionSpec as P

HIGHEST = lax.Precision.HIGHEST
VMEM = pl.BlockSpec(memory_space=pltpu.VMEM)
NT = (((1,), (1,)), ((), ()))
CHUNKS = 1


def dot(a, b):
    return jnp.dot(a, b, precision=HIGHEST, preferred_element_type=jnp.float32)


def exchange(value, axes):
    return lax.all_to_all(value, axes, 0, 0, tiled=True)


def packed(value):
    half = value.shape[-2] // 2
    return jnp.concatenate([value[..., :half, :], value[..., half:, :]], axis=-1)


def unpacked(value):
    return jnp.concatenate([value[..., :64], value[..., 64:]], axis=-2)


def call(body, out, *args, specs=None, scratch=(), limit=32 << 20):
    return pl.pallas_call(
        body,
        out_shape=out,
        in_specs=specs or [VMEM] * len(args),
        out_specs=jax.tree.map(lambda _: VMEM, out),
        scratch_shapes=scratch,
        compiler_params=pltpu.CompilerParams(vmem_limit_bytes=limit),
    )(*args)


def f32(*shape):
    return jax.ShapeDtypeStruct(shape, jnp.float32)


def two_parts(value):
    high = value.astype(jnp.bfloat16)
    low = (value - high.astype(jnp.float32)).astype(jnp.bfloat16)
    return jnp.concatenate([high, low], axis=0)


def permuted(value, source_of):
    row = lax.broadcasted_iota(jnp.int32, (128, 128), 0)
    lane = lax.broadcasted_iota(jnp.int32, (128, 128), 1)
    return dot(value, (row == source_of(lane)).astype(jnp.float32))


def staggered(value, step, shift=0):
    row = lax.broadcasted_iota(jnp.int32, value.shape, 0) % (128 // (step % 128 & -(step % 128)))
    out = value
    for i in range(128 // (step % 128 & -(step % 128))):
        turn = (shift + step * i) % 128
        out = jnp.where(row == i, pltpu.roll(value, turn, 1) if turn else value, out)
    return out


def start_body(panel_hbm, solved_hbm, sketch_hbm, inverses_hbm, coupling_hbm, out, *held):
    inverses, coupling, sketch, panel, solved_t, sems = held
    pairs = [(inverses_hbm, inverses), (coupling_hbm, coupling), (sketch_hbm, sketch)]
    for k in range(CHUNKS):
        span = pl.ds(k * (4096 // CHUNKS), 4096 // CHUNKS)
        pairs += [(solved_hbm.at[:, span], solved_t.at[k]), (panel_hbm.at[:, span], panel.at[k])]
    copies = [
        pltpu.make_async_copy(source, target, sems.at[k])
        for k, (source, target) in enumerate(pairs)
    ]
    for copy in copies:
        copy.start()

    copies[0].wait()
    both = jnp.concatenate([inverses[1], inverses[0]], axis=0)
    both = permuted(both, lambda m: 32 * (m % 16 // 4) + 4 * (m // 16) + m % 4)
    both = staggered(both, 16)
    group = lax.broadcasted_iota(jnp.int32, (32, 128), 1) // 16
    row = lax.broadcasted_iota(jnp.int32, (32, 128), 0)
    for c2 in range(8):
        kept = jnp.where(group == (c2 + row) % 8, both, 0.0)
        kept = kept.reshape(4, 8, 128).sum(axis=1)
        for x2 in range(4):
            out[8 * x2 + c2, 2:6] = kept

    copies[1].wait()
    couple = permuted(
        coupling[...], lambda m: 64 * (m % 16 // 8) + 16 * (m // 32) + 8 * (m % 32 // 16) + m % 8
    )
    couple = staggered(couple, 32)
    group = group[:16] // 2
    row = row[:16]
    for x2 in range(4):
        kept = jnp.where(group == (x2 + row) % 4, couple, 0.0)
        for g in range(4):
            piece = jnp.sum(jnp.where(row // 4 == g, kept, 0.0), axis=0, keepdims=True)
            out[8 * x2 + g, 6:7] = piece
            out[8 * x2 + 4 + g, 6:7] = piece
            out[8 * x2 + g, 7:8] = piece
            out[8 * x2 + 4 + g, 7:8] = piece

    copies[2].wait()
    products = jnp.zeros((64, 128), jnp.float32)
    for k in range(CHUNKS):
        copies[3 + 2 * k].wait()
        copies[4 + 2 * k].wait()
        products += lax.dot_general(
            two_parts(panel[k]), two_parts(solved_t[k]), NT, preferred_element_type=jnp.float32
        )
    total = products[:32] + products[32:]
    total = total[:, :64] + total[:, 64:]
    total = jnp.where(lax.axis_index("c") == 0, sketch[...], 0.0) - total
    for c2 in range(8):
        piece = packed(total[4 * c2 : 4 * c2 + 4])
        for x2 in range(4):
            out[8 * x2 + c2, 0:2] = piece


def split_body(got, out):
    x, c = lax.axis_index("x"), lax.axis_index("c")
    right = [unpacked(got[8 * k : 8 * k + 8, 0:2].sum(axis=0)) for k in range(4)]
    right = jnp.concatenate(
        [jnp.concatenate(right[:2], axis=0), jnp.concatenate(right[2:], axis=0)], axis=1
    )
    group = lax.broadcasted_iota(jnp.int32, (8, 128), 1) // 16
    row = lax.broadcasted_iota(jnp.int32, (8, 128), 0)

    mats = [jnp.zeros((8, 128), jnp.float32) for _ in range(4)]
    for c1 in range(8):
        piece = got[8 * x + c1, 2:6]
        piece = pltpu.roll(piece, (16 * (c1 + 8) - 16 * c) % 128, 1)
        for k in range(4):
            mats[k] = jnp.where(group == (c1 + row) % 8, piece[k : k + 1], mats[k])
    mats = [staggered(mat, -16) for mat in mats]

    halves = [jnp.zeros((8, 128), jnp.float32) for _ in range(2)]
    for a in range(2):
        for c1 in range(8):
            piece = got[8 * (c // 4 + 2 * a) + c1, 6:8]
            piece = pltpu.roll(piece, (16 * c1 + 128 - 32 * x) % 128, 1)[:1]
            for h in range(2):
                here = (group == (2 * row + h + c1) % 8) & (row // 4 == a)
                halves[h] = jnp.where(here, piece, halves[h])
    halves = [staggered(half, -32, -16 * h) for h, half in enumerate(halves)]

    own = got[pl.ds(pl.multiple_of(8 * x, 8), 8), 0:2].sum(axis=0)
    for h in range(2):
        near = jnp.concatenate([mats[h][:, :64], mats[2 + h][:, :64]], axis=1)
        far = jnp.concatenate([mats[h][:, 64:], mats[2 + h][:, 64:]], axis=1)
        near = jnp.where(lax.axis_index("zh") < 4, near, right)
        piece = own[:, 64 * h : 64 * h + 64]
        piece = jnp.concatenate([piece[0:1], piece[1:2]], axis=1)
        piece = jnp.concatenate([piece, piece], axis=0)
        for k in range(8):
            for m, tile in enumerate((near, far, halves[h])):
                for j in range(4):
                    out[2 * k + h, 4 * m + j] = tile[2 * j : 2 * j + 2]
            out[2 * k + h, 12] = piece


def applied(got, lanes, vector):
    terms = dot(got[:, 8:16, lanes].reshape(128, 64), vector[64:])
    near = dot(got[0:8, 0:8, lanes].reshape(64, 64), vector[:64])
    return jnp.concatenate([terms[:64] + near, terms[64:]], axis=0)


def last_body(got, out):
    right = unpacked(got[8:16, 0:8]).reshape(128, 64)
    terms = packed(applied(got, slice(0, 64), right))
    for k in range(8):
        out[k] = terms


def bent_body(parts, got, out, y_out):
    y_last = unpacked(parts[...].sum(axis=0))
    bent = dot(got[:, 16:24].reshape(128, 128), y_last).reshape(8, 2, 8, 64)
    bent = jnp.concatenate([bent[:, 0].reshape(64, 64), bent[:, 1].reshape(64, 64)], axis=1)

    x, h = lax.axis_index("x"), lax.axis_index("zl")
    row = lax.broadcasted_iota(jnp.int32, (8, 128), 0)
    half = lax.broadcasted_iota(jnp.int32, (8, 128), 1) // 64
    here = (half == x // 2) & (row // 2 == 2 * (x % 2) + h)
    rows = []
    for z in range(8):
        piece = got[z, 24:25]
        piece = jnp.where(row % 2 == x // 2, piece, pltpu.roll(piece, 64, 1))
        rows.append(jnp.where(here, piece, 0.0))
    terms = jnp.concatenate(rows, axis=0) - bent
    for k in range(8):
        out[k] = terms
    for g in range(4):
        y_out[g] = packed(y_last[32 * g : 32 * g + 32])


def first_body(parts, y_last, got, out):
    right = unpacked(parts[...].sum(axis=0).reshape(8, 8, 128)).reshape(128, 64)
    terms = applied(got, slice(64, 128), right)
    for g in range(4):
        piece = packed(terms[32 * g : 32 * g + 32])
        last = y_last[g]
        for k in range(8):
            out[8 * k + g] = piece
            out[8 * k + 4 + g] = last


def design_body(parts, design, out, held):
    c = lax.axis_index("c")
    for h in range(2):
        for x in range(4):
            k = 4 * h + x
            piece = parts[8 * k : 8 * k + 8].sum(axis=0)
            piece = jnp.where(c < 4, piece, parts[8 * k])
            for z in range(4):
                row = 64 * z + 16 * x + 8 * h
                held[row : row + 8, :] = piece[
                    8 * (z % 2) : 8 * (z % 2) + 8, 64 * (z // 2) : 64 * (z // 2) + 64
                ]
    turned = held[...].T.astype(jnp.bfloat16)
    own = 32 * (4 * lax.axis_index("zl") + lax.axis_index("x"))
    own = held[pl.ds(pl.multiple_of(own, 32), 32), :]
    own = jnp.concatenate([own[8 * k : 8 * k + 8] for k in range(4)], axis=1)
    for k in range(8):
        out[k, :64] = lax.dot_general(
            turned, design[256 * k : 256 * k + 256], NT, preferred_element_type=jnp.float32
        )
        out[k, 64:] = own


def leverage_body(got, prior_t, solution_rows, leverage):
    total = prior_t[...] + got[:, :64].sum(axis=0)
    leverage[...] = jnp.sum(total * total, axis=0, keepdims=True) * (1.0 / 64)
    own = got[lax.axis_index("zh"), 64:72]
    for k in range(4):
        solution_rows[8 * k : 8 * k + 8, :] = own[:, 64 * k : 64 * k + 64]


def local(panel, solved, sketch, inverses, coupling, design, prior):
    message = call(
        start_body,
        f32(32, 8, 128),
        *(
            pltpu.with_memory_space_constraint(value, pltpu.HBM)
            for value in (panel, solved.T, sketch, inverses, coupling)
        ),
        specs=[pl.BlockSpec(memory_space=pl.ANY)] * 5,
        scratch=[
            pltpu.VMEM((2, 16, 128), jnp.float32),
            pltpu.VMEM((16, 128), jnp.float32),
            pltpu.VMEM((32, 64), jnp.float32),
            pltpu.VMEM((CHUNKS, 32, 4096 // CHUNKS), jnp.float32),
            pltpu.VMEM((CHUNKS, 64, 4096 // CHUNKS), jnp.float32),
            pltpu.SemaphoreType.DMA((3 + 2 * CHUNKS,)),
        ],
    )
    got = exchange(message, ("x", "c"))

    got = exchange(call(split_body, f32(16, 13, 2, 128), got), ("zh", "zl")).reshape(16, 26, 128)

    parts = exchange(call(last_body, f32(8, 64, 128), got), "c")

    bent, y_last = call(bent_body, (f32(8, 64, 128), f32(4, 16, 128)), parts, got)
    parts = exchange(bent, ("zl", "x"))

    parts = exchange(call(first_body, f32(64, 16, 128), parts, y_last, got), ("zl", "x", "c"))

    message = call(
        design_body, f32(8, 72, 256), parts, design, scratch=[pltpu.VMEM((256, 64), jnp.float32)]
    )
    got = exchange(message, "c")
    block_solution, leverage = call(leverage_body, (f32(32, 64), f32(1, 256)), got, prior.T)
    return block_solution, leverage.reshape(256)


def solution(mesh):
    fine = Mesh(mesh.devices.reshape(8, 2, 4, 8), ("zh", "zl", "x", "c"))
    r = ("zh", "zl", "x")
    in_specs = (
        P(r, "c"),
        P("c", None),
        P(r, None),
        P(None, r, "c"),
        P(r, "c"),
        P(r, "c"),
        P((*r, "c"), None),
    )
    out_specs = (P(r, None), P((*r, "c")))
    return jax.shard_map(local, mesh=fine, in_specs=in_specs, out_specs=out_specs, check_vma=False)
```

```python
import jax
import jax.numpy as jnp
from jax import lax
from jax.experimental import pallas as pl
from jax.experimental.pallas import tpu as pltpu
from jax.sharding import Mesh
from jax.sharding import PartitionSpec as P

HIGHEST = lax.Precision.HIGHEST
VMEM = pl.BlockSpec(memory_space=pltpu.VMEM)
NT = (((1,), (1,)), ((), ()))
CHUNKS = 1


def dot(a, b):
    return jnp.dot(a, b, precision=HIGHEST, preferred_element_type=jnp.float32)


def exchange(value, axes):
    return lax.all_to_all(value, axes, 0, 0, tiled=True)


def packed(value):
    half = value.shape[-2] // 2
    return jnp.concatenate([value[..., :half, :], value[..., half:, :]], axis=-1)


def unpacked(value):
    return jnp.concatenate([value[..., :64], value[..., 64:]], axis=-2)


def call(body, out, *args, specs=None, scratch=(), limit=32 << 20):
    return pl.pallas_call(
        body,
        out_shape=out,
        in_specs=specs or [VMEM] * len(args),
        out_specs=jax.tree.map(lambda _: VMEM, out),
        scratch_shapes=scratch,
        compiler_params=pltpu.CompilerParams(vmem_limit_bytes=limit),
    )(*args)


def f32(*shape):
    return jax.ShapeDtypeStruct(shape, jnp.float32)


def two_parts(value):
    high = value.astype(jnp.bfloat16)
    low = (value - high.astype(jnp.float32)).astype(jnp.bfloat16)
    return jnp.concatenate([high, low], axis=0)


def permuted(value, source_of):
    row = lax.broadcasted_iota(jnp.int32, (128, 128), 0)
    lane = lax.broadcasted_iota(jnp.int32, (128, 128), 1)
    return dot(value, (row == source_of(lane)).astype(jnp.float32))


def staggered(value, step, shift=0):
    row = lax.broadcasted_iota(jnp.int32, value.shape, 0) % (128 // (step % 128 & -(step % 128)))
    out = value
    for i in range(128 // (step % 128 & -(step % 128))):
        turn = (shift + step * i) % 128
        out = jnp.where(row == i, pltpu.roll(value, turn, 1) if turn else value, out)
    return out


def start_body(panel_hbm, solved_hbm, sketch_hbm, inverses_hbm, coupling_hbm, out, *held):
    inverses, coupling, sketch, panel, solved_t, sems = held
    pairs = [(inverses_hbm, inverses), (coupling_hbm, coupling), (sketch_hbm, sketch)]
    for k in range(CHUNKS):
        span = pl.ds(k * (4096 // CHUNKS), 4096 // CHUNKS)
        pairs += [(solved_hbm.at[:, span], solved_t.at[k]), (panel_hbm.at[:, span], panel.at[k])]
    copies = [
        pltpu.make_async_copy(source, target, sems.at[k])
        for k, (source, target) in enumerate(pairs)
    ]
    for copy in copies:
        copy.start()

    copies[0].wait()
    both = jnp.concatenate([inverses[1], inverses[0]], axis=0)
    both = permuted(both, lambda m: 32 * (m % 16 // 4) + 4 * (m // 16) + m % 4)
    both = staggered(both, 16)
    group = lax.broadcasted_iota(jnp.int32, (32, 128), 1) // 16
    row = lax.broadcasted_iota(jnp.int32, (32, 128), 0)
    for c2 in range(8):
        kept = jnp.where(group == (c2 + row) % 8, both, 0.0)
        kept = kept.reshape(4, 8, 128).sum(axis=1)
        for x2 in range(4):
            out[8 * x2 + c2, 2:6] = kept

    copies[1].wait()
    couple = permuted(
        coupling[...], lambda m: 64 * (m % 16 // 8) + 16 * (m // 32) + 8 * (m % 32 // 16) + m % 8
    )
    couple = staggered(couple, 32)
    group = group[:16] // 2
    row = row[:16]
    for x2 in range(4):
        kept = jnp.where(group == (x2 + row) % 4, couple, 0.0)
        for g in range(4):
            piece = jnp.sum(jnp.where(row // 4 == g, kept, 0.0), axis=0, keepdims=True)
            out[8 * x2 + g, 6:7] = piece
            out[8 * x2 + 4 + g, 6:7] = piece
            out[8 * x2 + g, 7:8] = piece
            out[8 * x2 + 4 + g, 7:8] = piece

    copies[2].wait()
    products = jnp.zeros((64, 128), jnp.float32)
    for k in range(CHUNKS):
        copies[3 + 2 * k].wait()
        copies[4 + 2 * k].wait()
        products += lax.dot_general(
            two_parts(panel[k]), two_parts(solved_t[k]), NT, preferred_element_type=jnp.float32
        )
    total = products[:32] + products[32:]
    total = total[:, :64] + total[:, 64:]
    total = jnp.where(lax.axis_index("c") == 0, sketch[...], 0.0) - total
    for c2 in range(8):
        piece = packed(total[4 * c2 : 4 * c2 + 4])
        for x2 in range(4):
            out[8 * x2 + c2, 0:2] = piece


def split_body(got, out):
    x, c = lax.axis_index("x"), lax.axis_index("c")
    right = [unpacked(got[8 * k : 8 * k + 8, 0:2].sum(axis=0)) for k in range(4)]
    right = jnp.concatenate(
        [jnp.concatenate(right[:2], axis=0), jnp.concatenate(right[2:], axis=0)], axis=1
    )
    group = lax.broadcasted_iota(jnp.int32, (8, 128), 1) // 16
    row = lax.broadcasted_iota(jnp.int32, (8, 128), 0)

    mats = [jnp.zeros((8, 128), jnp.float32) for _ in range(4)]
    for c1 in range(8):
        piece = got[8 * x + c1, 2:6]
        piece = pltpu.roll(piece, (16 * (c1 + 8) - 16 * c) % 128, 1)
        for k in range(4):
            mats[k] = jnp.where(group == (c1 + row) % 8, piece[k : k + 1], mats[k])
    mats = [staggered(mat, -16) for mat in mats]

    halves = [jnp.zeros((8, 128), jnp.float32) for _ in range(2)]
    for a in range(2):
        for c1 in range(8):
            piece = got[8 * (c // 4 + 2 * a) + c1, 6:8]
            piece = pltpu.roll(piece, (16 * c1 + 128 - 32 * x) % 128, 1)[:1]
            for h in range(2):
                here = (group == (2 * row + h + c1) % 8) & (row // 4 == a)
                halves[h] = jnp.where(here, piece, halves[h])
    halves = [staggered(half, -32, -16 * h) for h, half in enumerate(halves)]

    own = got[pl.ds(pl.multiple_of(8 * x, 8), 8), 0:2].sum(axis=0)
    for h in range(2):
        near = jnp.concatenate([mats[h][:, :64], mats[2 + h][:, :64]], axis=1)
        far = jnp.concatenate([mats[h][:, 64:], mats[2 + h][:, 64:]], axis=1)
        near = jnp.where(lax.axis_index("zh") < 4, near, right)
        piece = own[:, 64 * h : 64 * h + 64]
        piece = jnp.concatenate([piece[0:1], piece[1:2]], axis=1)
        piece = jnp.concatenate([piece, piece], axis=0)
        for k in range(8):
            for m, tile in enumerate((near, far, halves[h])):
                for j in range(4):
                    out[2 * k + h, 4 * m + j] = tile[2 * j : 2 * j + 2]
            out[2 * k + h, 12] = piece


def applied(got, lanes, vector):
    terms = dot(got[:, 8:16, lanes].reshape(128, 64), vector[64:])
    near = dot(got[0:8, 0:8, lanes].reshape(64, 64), vector[:64])
    return jnp.concatenate([terms[:64] + near, terms[64:]], axis=0)


def last_body(got, out):
    right = unpacked(got[8:16, 0:8]).reshape(128, 64)
    terms = packed(applied(got, slice(0, 64), right))
    for k in range(8):
        out[k] = terms


def bent_body(parts, got, out, y_out):
    y_last = unpacked(parts[...].sum(axis=0))
    bent = dot(got[:, 16:24].reshape(128, 128), y_last).reshape(8, 2, 8, 64)
    bent = jnp.concatenate([bent[:, 0].reshape(64, 64), bent[:, 1].reshape(64, 64)], axis=1)

    x, h = lax.axis_index("x"), lax.axis_index("zl")
    row = lax.broadcasted_iota(jnp.int32, (8, 128), 0)
    half = lax.broadcasted_iota(jnp.int32, (8, 128), 1) // 64
    here = (half == x // 2) & (row // 2 == 2 * (x % 2) + h)
    rows = []
    for z in range(8):
        piece = got[z, 24:25]
        piece = jnp.where(row % 2 == x // 2, piece, pltpu.roll(piece, 64, 1))
        rows.append(jnp.where(here, piece, 0.0))
    terms = jnp.concatenate(rows, axis=0) - bent
    for k in range(8):
        out[k] = terms
    for g in range(4):
        y_out[g] = packed(y_last[32 * g : 32 * g + 32])


def first_body(parts, got, out):
    right = unpacked(parts[...].sum(axis=0).reshape(8, 8, 128)).reshape(128, 64)
    terms = applied(got, slice(64, 128), right)
    pieces = [packed(terms[32 * g : 32 * g + 32]) for g in range(4)]
    block = lax.axis_index("zh") % 4
    shown = pieces[0]
    for g in range(1, 4):
        shown = jnp.where(block == g, pieces[g], shown)
    for k in range(8):
        out[k, 0:16] = pieces[k % 4]
        out[k, 16:32] = shown


def own_body(parts, y_last, out):
    c, zh = lax.axis_index("c"), lax.axis_index("zh")
    total = parts[...].sum(axis=0)
    piece = jnp.where(c < 4, total[:16], y_last[c % 4])
    shown = jnp.where(zh < 4, total[16:], y_last[zh % 4])
    for k in range(8):
        out[k, 0:16] = piece
        half = k % 4 // 2
        out[k, 16:24] = shown[8 * half : 8 * half + 8]


def design_body(parts, design, out, solution_rows, held):
    for h in range(2):
        for x in range(4):
            piece = parts[4 * h + x, 0:16]
            for z in range(4):
                row = 64 * z + 16 * x + 8 * h
                held[row : row + 8, :] = piece[
                    8 * (z % 2) : 8 * (z % 2) + 8, 64 * (z // 2) : 64 * (z // 2) + 64
                ]
    turned = held[...].T.astype(jnp.bfloat16)
    for k in range(8):
        out[k] = lax.dot_general(
            turned, design[256 * k : 256 * k + 256], NT, preferred_element_type=jnp.float32
        )
    x, zl = lax.axis_index("x"), lax.axis_index("zl")
    for b in range(2):
        for h in range(2):
            piece = parts[4 * h + 2 * (x % 2) + b, 16:24]
            row = 16 * b + 8 * h
            solution_rows[row : row + 8, :] = jnp.where(zl == 0, piece[:, :64], piece[:, 64:])


def leverage_body(got, prior_t, leverage):
    total = prior_t[...] + got[...].sum(axis=0)
    leverage[...] = jnp.sum(total * total, axis=0, keepdims=True) * (1.0 / 64)


def local(panel, solved, sketch, inverses, coupling, design, prior):
    message = call(
        start_body,
        f32(32, 8, 128),
        *(
            pltpu.with_memory_space_constraint(value, pltpu.HBM)
            for value in (panel, solved.T, sketch, inverses, coupling)
        ),
        specs=[pl.BlockSpec(memory_space=pl.ANY)] * 5,
        scratch=[
            pltpu.VMEM((2, 16, 128), jnp.float32),
            pltpu.VMEM((16, 128), jnp.float32),
            pltpu.VMEM((32, 64), jnp.float32),
            pltpu.VMEM((CHUNKS, 32, 4096 // CHUNKS), jnp.float32),
            pltpu.VMEM((CHUNKS, 64, 4096 // CHUNKS), jnp.float32),
            pltpu.SemaphoreType.DMA((3 + 2 * CHUNKS,)),
        ],
    )
    got = exchange(message, ("x", "c"))

    got = exchange(call(split_body, f32(16, 13, 2, 128), got), ("zh", "zl")).reshape(16, 26, 128)

    parts = exchange(call(last_body, f32(8, 64, 128), got), "c")

    bent, y_last = call(bent_body, (f32(8, 64, 128), f32(4, 16, 128)), parts, got)
    parts = exchange(bent, ("zl", "x"))

    parts = exchange(call(first_body, f32(8, 32, 128), parts, got), "c")
    parts = exchange(call(own_body, f32(8, 24, 128), parts, y_last), ("zl", "x"))

    message, block_solution = call(
        design_body,
        (f32(8, 64, 256), f32(32, 64)),
        parts,
        design,
        scratch=[pltpu.VMEM((256, 64), jnp.float32)],
    )
    leverage = call(leverage_body, f32(1, 256), exchange(message, "c"), prior.T)
    return block_solution, leverage.reshape(256)


def solution(mesh):
    fine = Mesh(mesh.devices.reshape(8, 2, 4, 8), ("zh", "zl", "x", "c"))
    r = ("zh", "zl", "x")
    in_specs = (
        P(r, "c"),
        P("c", None),
        P(r, None),
        P(None, r, "c"),
        P(r, "c"),
        P(r, "c"),
        P((*r, "c"), None),
    )
    out_specs = (P(r, None), P((*r, "c")))
    return jax.shard_map(local, mesh=fine, in_specs=in_specs, out_specs=out_specs, check_vma=False)
```

```python
import jax
import jax.numpy as jnp
from jax import lax
from jax.experimental import pallas as pl
from jax.experimental.pallas import tpu as pltpu
from jax.sharding import Mesh
from jax.sharding import PartitionSpec as P

HIGHEST = lax.Precision.HIGHEST
VMEM = pl.BlockSpec(memory_space=pltpu.VMEM)
NT = (((1,), (1,)), ((), ()))
CHUNKS = 1


def dot(a, b):
    return jnp.dot(a, b, precision=HIGHEST, preferred_element_type=jnp.float32)


def exchange(value, axes):
    return lax.all_to_all(value, axes, 0, 0, tiled=True)


def packed(value):
    half = value.shape[-2] // 2
    return jnp.concatenate([value[..., :half, :], value[..., half:, :]], axis=-1)


def unpacked(value):
    return jnp.concatenate([value[..., :64], value[..., 64:]], axis=-2)


def call(body, out, *args, specs=None, scratch=(), limit=32 << 20):
    return pl.pallas_call(
        body,
        out_shape=out,
        in_specs=specs or [VMEM] * len(args),
        out_specs=jax.tree.map(lambda _: VMEM, out),
        scratch_shapes=scratch,
        compiler_params=pltpu.CompilerParams(vmem_limit_bytes=limit),
    )(*args)


def f32(*shape):
    return jax.ShapeDtypeStruct(shape, jnp.float32)


def two_parts(value):
    high = value.astype(jnp.bfloat16)
    low = (value - high.astype(jnp.float32)).astype(jnp.bfloat16)
    return jnp.concatenate([high, low], axis=0)


def permuted(value, source_of):
    row = lax.broadcasted_iota(jnp.int32, (128, 128), 0)
    lane = lax.broadcasted_iota(jnp.int32, (128, 128), 1)
    return dot(value, (row == source_of(lane)).astype(jnp.float32))


def staggered(value, step, shift=0):
    row = lax.broadcasted_iota(jnp.int32, value.shape, 0) % (128 // (step % 128 & -(step % 128)))
    out = value
    for i in range(128 // (step % 128 & -(step % 128))):
        turn = (shift + step * i) % 128
        out = jnp.where(row == i, pltpu.roll(value, turn, 1) if turn else value, out)
    return out


def start_body(panel_hbm, solved_hbm, sketch_hbm, inverses_hbm, coupling_hbm, out, *held):
    inverses, coupling, sketch, panel, solved_t, sems = held
    pairs = [(inverses_hbm, inverses), (coupling_hbm, coupling), (sketch_hbm, sketch)]
    for k in range(CHUNKS):
        span = pl.ds(k * (4096 // CHUNKS), 4096 // CHUNKS)
        pairs += [(solved_hbm.at[:, span], solved_t.at[k]), (panel_hbm.at[:, span], panel.at[k])]
    copies = [
        pltpu.make_async_copy(source, target, sems.at[k])
        for k, (source, target) in enumerate(pairs)
    ]
    for copy in copies:
        copy.start()

    copies[0].wait()
    both = jnp.concatenate([inverses[1], inverses[0]], axis=0)
    both = permuted(both, lambda m: 32 * (m % 16 // 4) + 4 * (m // 16) + m % 4)
    both = staggered(both, 16)
    group = lax.broadcasted_iota(jnp.int32, (32, 128), 1) // 16
    row = lax.broadcasted_iota(jnp.int32, (32, 128), 0)
    for c2 in range(8):
        kept = jnp.where(group == (c2 + row) % 8, both, 0.0)
        kept = kept.reshape(4, 8, 128).sum(axis=1)
        for x2 in range(4):
            out[8 * x2 + c2, 2:6] = kept

    copies[1].wait()
    couple = permuted(
        coupling[...], lambda m: 64 * (m % 16 // 8) + 16 * (m // 32) + 8 * (m % 32 // 16) + m % 8
    )
    couple = staggered(couple, 32)
    group = group[:16] // 2
    row = row[:16]
    for x2 in range(4):
        kept = jnp.where(group == (x2 + row) % 4, couple, 0.0)
        for g in range(4):
            piece = jnp.sum(jnp.where(row // 4 == g, kept, 0.0), axis=0, keepdims=True)
            out[8 * x2 + g, 6:7] = piece
            out[8 * x2 + 4 + g, 6:7] = piece
            out[8 * x2 + g, 7:8] = piece
            out[8 * x2 + 4 + g, 7:8] = piece

    copies[2].wait()
    products = jnp.zeros((64, 128), jnp.float32)
    for k in range(CHUNKS):
        copies[3 + 2 * k].wait()
        copies[4 + 2 * k].wait()
        products += lax.dot_general(
            two_parts(panel[k]), two_parts(solved_t[k]), NT, preferred_element_type=jnp.float32
        )
    total = products[:32] + products[32:]
    total = total[:, :64] + total[:, 64:]
    total = jnp.where(lax.axis_index("c") == 0, sketch[...], 0.0) - total
    for c2 in range(8):
        piece = packed(total[4 * c2 : 4 * c2 + 4])
        for x2 in range(4):
            out[8 * x2 + c2, 0:2] = piece


def split_body(got, out):
    x, c = lax.axis_index("x"), lax.axis_index("c")
    right = [unpacked(got[8 * k : 8 * k + 8, 0:2].sum(axis=0)) for k in range(4)]
    right = jnp.concatenate(
        [jnp.concatenate(right[:2], axis=0), jnp.concatenate(right[2:], axis=0)], axis=1
    )
    group = lax.broadcasted_iota(jnp.int32, (8, 128), 1) // 16
    row = lax.broadcasted_iota(jnp.int32, (8, 128), 0)

    mats = [jnp.zeros((8, 128), jnp.float32) for _ in range(4)]
    for c1 in range(8):
        piece = got[8 * x + c1, 2:6]
        piece = pltpu.roll(piece, (16 * (c1 + 8) - 16 * c) % 128, 1)
        for k in range(4):
            mats[k] = jnp.where(group == (c1 + row) % 8, piece[k : k + 1], mats[k])
    mats = [staggered(mat, -16) for mat in mats]

    halves = [jnp.zeros((8, 128), jnp.float32) for _ in range(2)]
    for a in range(2):
        for c1 in range(8):
            piece = got[8 * (c // 4 + 2 * a) + c1, 6:8]
            piece = pltpu.roll(piece, (16 * c1 + 128 - 32 * x) % 128, 1)[:1]
            for h in range(2):
                here = (group == (2 * row + h + c1) % 8) & (row // 4 == a)
                halves[h] = jnp.where(here, piece, halves[h])
    halves = [staggered(half, -32, -16 * h) for h, half in enumerate(halves)]

    own = got[pl.ds(pl.multiple_of(8 * x, 8), 8), 0:2].sum(axis=0)
    for h in range(2):
        near = jnp.concatenate([mats[h][:, :64], mats[2 + h][:, :64]], axis=1)
        far = jnp.concatenate([mats[h][:, 64:], mats[2 + h][:, 64:]], axis=1)
        near = jnp.where(lax.axis_index("zh") < 4, near, right)
        piece = own[:, 64 * h : 64 * h + 64]
        piece = jnp.concatenate([piece[0:1], piece[1:2]], axis=1)
        piece = jnp.concatenate([piece, piece], axis=0)
        for k in range(8):
            for m, tile in enumerate((near, far, halves[h])):
                for j in range(4):
                    out[2 * k + h, 4 * m + j] = tile[2 * j : 2 * j + 2]
            out[2 * k + h, 12] = piece


def applied(got, lanes, vector):
    terms = dot(got[:, 8:16, lanes].reshape(128, 64), vector[64:])
    near = dot(got[0:8, 0:8, lanes].reshape(64, 64), vector[:64])
    return jnp.concatenate([terms[:64] + near, terms[64:]], axis=0)


def last_body(got, out):
    right = unpacked(got[8:16, 0:8]).reshape(128, 64)
    terms = packed(applied(got, slice(0, 64), right))
    for k in range(8):
        out[k] = terms


def bent_body(parts, got, out, y_out):
    y_last = unpacked(parts[...].sum(axis=0))
    bent = dot(got[:, 16:24].reshape(128, 128), y_last).reshape(8, 2, 8, 64)
    bent = jnp.concatenate([bent[:, 0].reshape(64, 64), bent[:, 1].reshape(64, 64)], axis=1)

    x, h = lax.axis_index("x"), lax.axis_index("zl")
    row = lax.broadcasted_iota(jnp.int32, (8, 128), 0)
    half = lax.broadcasted_iota(jnp.int32, (8, 128), 1) // 64
    here = (half == x // 2) & (row // 2 == 2 * (x % 2) + h)
    rows = []
    for z in range(8):
        piece = got[z, 24:25]
        piece = jnp.where(row % 2 == x // 2, piece, pltpu.roll(piece, 64, 1))
        rows.append(jnp.where(here, piece, 0.0))
    terms = jnp.concatenate(rows, axis=0) - bent
    for k in range(8):
        out[k] = terms
    for g in range(4):
        y_out[g] = packed(y_last[32 * g : 32 * g + 32])


def first_body(parts, got, out):
    right = unpacked(parts[...].sum(axis=0).reshape(8, 8, 128)).reshape(128, 64)
    terms = applied(got, slice(64, 128), right)
    pieces = [packed(terms[32 * g : 32 * g + 32]) for g in range(4)]
    block = lax.axis_index("zh") % 4
    shown = pieces[0]
    for g in range(1, 4):
        shown = jnp.where(block == g, pieces[g], shown)
    for k in range(8):
        out[k, 0:16] = pieces[k % 4]
        out[k, 16:32] = shown


def own_body(parts, y_last, out):
    c, zh = lax.axis_index("c"), lax.axis_index("zh")
    total = parts[...].sum(axis=0)
    piece = jnp.where(c < 4, total[:16], y_last[c % 4])
    shown = jnp.where(zh < 4, total[16:], y_last[zh % 4])
    for k in range(8):
        out[k, 0:16] = piece
        half = k % 4 // 2
        out[k, 16:24] = shown[8 * half : 8 * half + 8]


def design_body(parts, design, out, held):
    for h in range(2):
        for x in range(4):
            piece = parts[4 * h + x, 0:16]
            for z in range(4):
                row = 64 * z + 16 * x + 8 * h
                held[row : row + 8, :] = piece[
                    8 * (z % 2) : 8 * (z % 2) + 8, 64 * (z // 2) : 64 * (z // 2) + 64
                ]
    turned = held[...].T.astype(jnp.bfloat16)
    for k in range(8):
        out[k] = lax.dot_general(
            turned, design[256 * k : 256 * k + 256], NT, preferred_element_type=jnp.float32
        )


def leverage_body(got, parts, prior_t, solution_rows, leverage):
    x, zl = lax.axis_index("x"), lax.axis_index("zl")
    for b in range(2):
        for h in range(2):
            piece = parts[4 * h + 2 * (x % 2) + b, 16:24]
            row = 16 * b + 8 * h
            solution_rows[row : row + 8, :] = jnp.where(zl == 0, piece[:, :64], piece[:, 64:])
    total = prior_t[...] + got[...].sum(axis=0)
    leverage[...] = jnp.sum(total * total, axis=0, keepdims=True) * (1.0 / 64)


def local(panel, solved, sketch, inverses, coupling, design, prior):
    message = call(
        start_body,
        f32(32, 8, 128),
        *(
            pltpu.with_memory_space_constraint(value, pltpu.HBM)
            for value in (panel, solved.T, sketch, inverses, coupling)
        ),
        specs=[pl.BlockSpec(memory_space=pl.ANY)] * 5,
        scratch=[
            pltpu.VMEM((2, 16, 128), jnp.float32),
            pltpu.VMEM((16, 128), jnp.float32),
            pltpu.VMEM((32, 64), jnp.float32),
            pltpu.VMEM((CHUNKS, 32, 4096 // CHUNKS), jnp.float32),
            pltpu.VMEM((CHUNKS, 64, 4096 // CHUNKS), jnp.float32),
            pltpu.SemaphoreType.DMA((3 + 2 * CHUNKS,)),
        ],
    )
    got = exchange(message, ("x", "c"))

    got = exchange(call(split_body, f32(16, 13, 2, 128), got), ("zh", "zl")).reshape(16, 26, 128)

    parts = exchange(call(last_body, f32(8, 64, 128), got), "c")

    bent, y_last = call(bent_body, (f32(8, 64, 128), f32(4, 16, 128)), parts, got)
    parts = exchange(bent, ("zl", "x"))

    parts = exchange(call(first_body, f32(8, 32, 128), parts, got), "c")
    parts = exchange(call(own_body, f32(8, 24, 128), parts, y_last), ("zl", "x"))

    message = call(
        design_body, f32(8, 64, 256), parts, design, scratch=[pltpu.VMEM((256, 64), jnp.float32)]
    )
    block_solution, leverage = call(
        leverage_body, (f32(32, 64), f32(1, 256)), exchange(message, "c"), parts, prior.T
    )
    return block_solution, leverage.reshape(256)


def solution(mesh):
    fine = Mesh(mesh.devices.reshape(8, 2, 4, 8), ("zh", "zl", "x", "c"))
    r = ("zh", "zl", "x")
    in_specs = (
        P(r, "c"),
        P("c", None),
        P(r, None),
        P(None, r, "c"),
        P(r, "c"),
        P(r, "c"),
        P((*r, "c"), None),
    )
    out_specs = (P(r, None), P((*r, "c")))
    return jax.shard_map(local, mesh=fine, in_specs=in_specs, out_specs=out_specs, check_vma=False)
```

```python
import jax
import jax.numpy as jnp
from jax import lax
from jax.experimental import pallas as pl
from jax.experimental.pallas import tpu as pltpu
from jax.sharding import Mesh
from jax.sharding import PartitionSpec as P

HIGHEST = lax.Precision.HIGHEST
VMEM = pl.BlockSpec(memory_space=pltpu.VMEM)
NT = (((1,), (1,)), ((), ()))
CHUNKS = 1


def dot(a, b):
    return jnp.dot(a, b, precision=HIGHEST, preferred_element_type=jnp.float32)


def exchange(value, axes):
    return lax.all_to_all(value, axes, 0, 0, tiled=True)


def packed(value):
    half = value.shape[-2] // 2
    return jnp.concatenate([value[..., :half, :], value[..., half:, :]], axis=-1)


def unpacked(value):
    return jnp.concatenate([value[..., :64], value[..., 64:]], axis=-2)


def call(body, out, *args, specs=None, scratch=(), limit=32 << 20):
    return pl.pallas_call(
        body,
        out_shape=out,
        in_specs=specs or [VMEM] * len(args),
        out_specs=jax.tree.map(lambda _: VMEM, out),
        scratch_shapes=scratch,
        compiler_params=pltpu.CompilerParams(vmem_limit_bytes=limit),
    )(*args)


def f32(*shape):
    return jax.ShapeDtypeStruct(shape, jnp.float32)


def two_parts(value):
    high = value.astype(jnp.bfloat16)
    low = (value - high.astype(jnp.float32)).astype(jnp.bfloat16)
    return jnp.concatenate([high, low], axis=0)


def permuted(value, source_of):
    row = lax.broadcasted_iota(jnp.int32, (128, 128), 0)
    lane = lax.broadcasted_iota(jnp.int32, (128, 128), 1)
    return dot(value, (row == source_of(lane)).astype(jnp.float32))


def staggered(value, step, shift=0):
    row = lax.broadcasted_iota(jnp.int32, value.shape, 0) % (128 // (step % 128 & -(step % 128)))
    out = value
    for i in range(128 // (step % 128 & -(step % 128))):
        turn = (shift + step * i) % 128
        out = jnp.where(row == i, pltpu.roll(value, turn, 1) if turn else value, out)
    return out


def start_body(panel_hbm, solved_hbm, sketch_hbm, inverses_hbm, coupling_hbm, out, *held):
    inverses, coupling, sketch, panel, solved_t, sems = held
    pairs = [(inverses_hbm, inverses), (coupling_hbm, coupling), (sketch_hbm, sketch)]
    for k in range(CHUNKS):
        span = pl.ds(k * (4096 // CHUNKS), 4096 // CHUNKS)
        pairs += [(solved_hbm.at[:, span], solved_t.at[k]), (panel_hbm.at[:, span], panel.at[k])]
    copies = [
        pltpu.make_async_copy(source, target, sems.at[k])
        for k, (source, target) in enumerate(pairs)
    ]
    for copy in copies:
        copy.start()

    copies[0].wait()
    both = jnp.concatenate([inverses[1], inverses[0]], axis=0)
    both = permuted(both, lambda m: 32 * (m % 16 // 4) + 4 * (m // 16) + m % 4)
    both = staggered(both, 16)
    group = lax.broadcasted_iota(jnp.int32, (32, 128), 1) // 16
    row = lax.broadcasted_iota(jnp.int32, (32, 128), 0)
    for c2 in range(8):
        kept = jnp.where(group == (c2 + row) % 8, both, 0.0)
        kept = kept.reshape(4, 8, 128).sum(axis=1)
        for x2 in range(4):
            out[8 * x2 + c2, 2:6] = kept

    copies[1].wait()
    couple = permuted(
        coupling[...], lambda m: 64 * (m % 16 // 8) + 16 * (m // 32) + 8 * (m % 32 // 16) + m % 8
    )
    couple = staggered(couple, 32)
    group = group[:16] // 2
    row = row[:16]
    for x2 in range(4):
        kept = jnp.where(group == (x2 + row) % 4, couple, 0.0)
        for g in range(4):
            piece = jnp.sum(jnp.where(row // 4 == g, kept, 0.0), axis=0, keepdims=True)
            out[8 * x2 + g, 6:7] = piece
            out[8 * x2 + 4 + g, 6:7] = piece
            out[8 * x2 + g, 7:8] = piece
            out[8 * x2 + 4 + g, 7:8] = piece

    copies[2].wait()
    products = jnp.zeros((64, 128), jnp.float32)
    for k in range(CHUNKS):
        copies[3 + 2 * k].wait()
        copies[4 + 2 * k].wait()
        products += lax.dot_general(
            two_parts(panel[k]), two_parts(solved_t[k]), NT, preferred_element_type=jnp.float32
        )
    total = products[:32] + products[32:]
    total = total[:, :64] + total[:, 64:]
    total = jnp.where(lax.axis_index("c") == 0, sketch[...], 0.0) - total
    for c2 in range(8):
        piece = packed(total[4 * c2 : 4 * c2 + 4])
        for x2 in range(4):
            out[8 * x2 + c2, 0:2] = piece


def split_body(got, out):
    x, c = lax.axis_index("x"), lax.axis_index("c")
    right = [unpacked(got[8 * k : 8 * k + 8, 0:2].sum(axis=0)) for k in range(4)]
    right = jnp.concatenate(
        [jnp.concatenate(right[:2], axis=0), jnp.concatenate(right[2:], axis=0)], axis=1
    )
    group = lax.broadcasted_iota(jnp.int32, (8, 128), 1) // 16
    row = lax.broadcasted_iota(jnp.int32, (8, 128), 0)

    mats = [jnp.zeros((8, 128), jnp.float32) for _ in range(4)]
    for c1 in range(8):
        piece = got[8 * x + c1, 2:6]
        piece = pltpu.roll(piece, (16 * (c1 + 8) - 16 * c) % 128, 1)
        for k in range(4):
            mats[k] = jnp.where(group == (c1 + row) % 8, piece[k : k + 1], mats[k])
    mats = [staggered(mat, -16) for mat in mats]

    halves = [jnp.zeros((8, 128), jnp.float32) for _ in range(2)]
    for a in range(2):
        for c1 in range(8):
            piece = got[8 * (c // 4 + 2 * a) + c1, 6:8]
            piece = pltpu.roll(piece, (16 * c1 + 128 - 32 * x) % 128, 1)[:1]
            for h in range(2):
                here = (group == (2 * row + h + c1) % 8) & (row // 4 == a)
                halves[h] = jnp.where(here, piece, halves[h])
    halves = [staggered(half, -32, -16 * h) for h, half in enumerate(halves)]

    own = got[pl.ds(pl.multiple_of(8 * x, 8), 8), 0:2].sum(axis=0)
    for h in range(2):
        near = jnp.concatenate([mats[h][:, :64], mats[2 + h][:, :64]], axis=1)
        far = jnp.concatenate([mats[h][:, 64:], mats[2 + h][:, 64:]], axis=1)
        near = jnp.where(lax.axis_index("zh") < 4, near, right)
        piece = own[:, 64 * h : 64 * h + 64]
        piece = jnp.concatenate([piece[0:1], piece[1:2]], axis=1)
        piece = jnp.concatenate([piece, piece], axis=0)
        for k in range(8):
            for m, tile in enumerate((near, far, halves[h])):
                for j in range(4):
                    out[2 * k + h, 4 * m + j] = tile[2 * j : 2 * j + 2]
            out[2 * k + h, 12] = piece


def applied(got, lanes, vector):
    terms = dot(got[:, 8:16, lanes].reshape(128, 64), vector[64:])
    near = dot(got[0:8, 0:8, lanes].reshape(64, 64), vector[:64])
    return jnp.concatenate([terms[:64] + near, terms[64:]], axis=0)


def last_body(got, out):
    right = unpacked(got[8:16, 0:8]).reshape(128, 64)
    terms = packed(applied(got, slice(0, 64), right))
    for k in range(8):
        out[k] = terms


def bent_body(parts, got, out, y_out):
    y_last = unpacked(parts[...].sum(axis=0))
    bent = dot(got[:, 16:24].reshape(128, 128), y_last).reshape(8, 2, 8, 64)
    bent = jnp.concatenate([bent[:, 0].reshape(64, 64), bent[:, 1].reshape(64, 64)], axis=1)

    x, h = lax.axis_index("x"), lax.axis_index("zl")
    row = lax.broadcasted_iota(jnp.int32, (8, 128), 0)
    half = lax.broadcasted_iota(jnp.int32, (8, 128), 1) // 64
    here = (half == x // 2) & (row // 2 == 2 * (x % 2) + h)
    rows = []
    for z in range(8):
        piece = got[z, 24:25]
        piece = jnp.where(row % 2 == x // 2, piece, pltpu.roll(piece, 64, 1))
        rows.append(jnp.where(here, piece, 0.0))
    terms = jnp.concatenate(rows, axis=0) - bent
    for k in range(8):
        out[k] = terms
    for g in range(4):
        y_out[g] = packed(y_last[32 * g : 32 * g + 32])


def first_body(parts, got, out):
    right = unpacked(parts[...].sum(axis=0).reshape(8, 8, 128)).reshape(128, 64)
    terms = applied(got, slice(64, 128), right)
    pieces = [packed(terms[32 * g : 32 * g + 32]) for g in range(4)]
    block = lax.axis_index("zh") % 4
    shown = pieces[0]
    for g in range(1, 4):
        shown = jnp.where(block == g, pieces[g], shown)
    for k in range(8):
        out[k, 0:16] = pieces[k % 4]
        out[k, 16:32] = shown


def own_body(parts, y_last, out):
    c, zh = lax.axis_index("c"), lax.axis_index("zh")
    total = parts[...].sum(axis=0)
    piece = jnp.where(c < 4, total[:16], y_last[c % 4])
    shown = jnp.where(zh < 4, total[16:], y_last[zh % 4])
    for k in range(8):
        out[k, 0:16] = piece
        half = k // 4
        out[k, 16:24] = shown[8 * half : 8 * half + 8]


def design_body(parts, design, out, held):
    for h in range(2):
        for x in range(4):
            piece = parts[2 * x + h, 0:16]
            for z in range(4):
                row = 64 * z + 16 * x + 8 * h
                held[row : row + 8, :] = piece[
                    8 * (z % 2) : 8 * (z % 2) + 8, 64 * (z // 2) : 64 * (z // 2) + 64
                ]
    turned = held[...].T.astype(jnp.bfloat16)
    for k in range(8):
        out[k] = lax.dot_general(
            turned, design[256 * k : 256 * k + 256], NT, preferred_element_type=jnp.float32
        )


def leverage_body(got, parts, prior_t, solution_rows, leverage):
    x, zl = lax.axis_index("x"), lax.axis_index("zl")
    for b in range(2):
        for h in range(2):
            piece = parts[4 * (x % 2) + 2 * b + h, 16:24]
            row = 16 * b + 8 * h
            solution_rows[row : row + 8, :] = jnp.where(zl == 0, piece[:, :64], piece[:, 64:])
    total = prior_t[...] + got[...].sum(axis=0)
    leverage[...] = jnp.sum(total * total, axis=0, keepdims=True) * (1.0 / 64)


def local(panel, solved, sketch, inverses, coupling, design, prior):
    message = call(
        start_body,
        f32(32, 8, 128),
        *(
            pltpu.with_memory_space_constraint(value, pltpu.HBM)
            for value in (panel, solved.T, sketch, inverses, coupling)
        ),
        specs=[pl.BlockSpec(memory_space=pl.ANY)] * 5,
        scratch=[
            pltpu.VMEM((2, 16, 128), jnp.float32),
            pltpu.VMEM((16, 128), jnp.float32),
            pltpu.VMEM((32, 64), jnp.float32),
            pltpu.VMEM((CHUNKS, 32, 4096 // CHUNKS), jnp.float32),
            pltpu.VMEM((CHUNKS, 64, 4096 // CHUNKS), jnp.float32),
            pltpu.SemaphoreType.DMA((3 + 2 * CHUNKS,)),
        ],
    )
    got = exchange(message, ("x", "c"))

    got = exchange(call(split_body, f32(16, 13, 2, 128), got), ("zh", "zl")).reshape(16, 26, 128)

    parts = exchange(call(last_body, f32(8, 64, 128), got), "c")

    bent, y_last = call(bent_body, (f32(8, 64, 128), f32(4, 16, 128)), parts, got)
    parts = exchange(bent, ("x", "zl"))

    parts = exchange(call(first_body, f32(8, 32, 128), parts, got), "c")
    parts = exchange(call(own_body, f32(8, 24, 128), parts, y_last), ("x", "zl"))

    message = call(
        design_body, f32(8, 64, 256), parts, design, scratch=[pltpu.VMEM((256, 64), jnp.float32)]
    )
    block_solution, leverage = call(
        leverage_body, (f32(32, 64), f32(1, 256)), exchange(message, "c"), parts, prior.T
    )
    return block_solution, leverage.reshape(256)


def solution(mesh):
    fine = Mesh(mesh.devices.reshape(8, 2, 4, 8), ("zh", "zl", "x", "c"))
    r = ("zh", "zl", "x")
    in_specs = (
        P(r, "c"),
        P("c", None),
        P(r, None),
        P(None, r, "c"),
        P(r, "c"),
        P(r, "c"),
        P((*r, "c"), None),
    )
    out_specs = (P(r, None), P((*r, "c")))
    return jax.shard_map(local, mesh=fine, in_specs=in_specs, out_specs=out_specs, check_vma=False)
```

```python
import jax
import jax.numpy as jnp
from jax import lax
from jax.experimental import pallas as pl
from jax.experimental.pallas import tpu as pltpu
from jax.sharding import Mesh
from jax.sharding import PartitionSpec as P

HIGHEST = lax.Precision.HIGHEST
VMEM = pl.BlockSpec(memory_space=pltpu.VMEM)
NT = (((1,), (1,)), ((), ()))
CHUNKS = 1


def dot(a, b):
    return jnp.dot(a, b, precision=HIGHEST, preferred_element_type=jnp.float32)


def exchange(value, axes):
    return lax.all_to_all(value, axes, 0, 0, tiled=True)


def packed(value):
    half = value.shape[-2] // 2
    return jnp.concatenate([value[..., :half, :], value[..., half:, :]], axis=-1)


def unpacked(value):
    return jnp.concatenate([value[..., :64], value[..., 64:]], axis=-2)


def call(body, out, *args, specs=None, scratch=(), limit=32 << 20):
    return pl.pallas_call(
        body,
        out_shape=out,
        in_specs=specs or [VMEM] * len(args),
        out_specs=jax.tree.map(lambda _: VMEM, out),
        scratch_shapes=scratch,
        compiler_params=pltpu.CompilerParams(vmem_limit_bytes=limit),
    )(*args)


def f32(*shape):
    return jax.ShapeDtypeStruct(shape, jnp.float32)


def two_parts(value):
    high = value.astype(jnp.bfloat16)
    low = (value - high.astype(jnp.float32)).astype(jnp.bfloat16)
    return jnp.concatenate([high, low], axis=0)


def permuted(value, source_of):
    row = lax.broadcasted_iota(jnp.int32, (128, 128), 0)
    lane = lax.broadcasted_iota(jnp.int32, (128, 128), 1)
    return dot(value, (row == source_of(lane)).astype(jnp.float32))


def staggered(value, step, shift=0):
    row = lax.broadcasted_iota(jnp.int32, value.shape, 0) % (128 // (step % 128 & -(step % 128)))
    out = value
    for i in range(128 // (step % 128 & -(step % 128))):
        turn = (shift + step * i) % 128
        out = jnp.where(row == i, pltpu.roll(value, turn, 1) if turn else value, out)
    return out


def start_body(panel_hbm, solved_hbm, sketch_hbm, inverses_hbm, coupling_hbm, out, *held):
    inverses, coupling, sketch, panel, solved_t, sems = held
    pairs = [(inverses_hbm, inverses), (coupling_hbm, coupling), (sketch_hbm, sketch)]
    for k in range(CHUNKS):
        span = pl.ds(k * (4096 // CHUNKS), 4096 // CHUNKS)
        pairs += [(solved_hbm.at[:, span], solved_t.at[k]), (panel_hbm.at[:, span], panel.at[k])]
    copies = [
        pltpu.make_async_copy(source, target, sems.at[k])
        for k, (source, target) in enumerate(pairs)
    ]
    for copy in copies:
        copy.start()

    copies[0].wait()
    both = jnp.concatenate([inverses[1], inverses[0]], axis=0)
    both = permuted(both, lambda m: 32 * (m % 16 // 4) + 4 * (m // 16) + m % 4)
    both = staggered(both, 16)
    group = lax.broadcasted_iota(jnp.int32, (32, 128), 1) // 16
    row = lax.broadcasted_iota(jnp.int32, (32, 128), 0)
    for c2 in range(8):
        kept = jnp.where(group == (c2 + row) % 8, both, 0.0)
        kept = kept.reshape(4, 8, 128).sum(axis=1)
        for x2 in range(4):
            out[8 * x2 + c2, 2:6] = kept

    copies[1].wait()
    couple = permuted(
        coupling[...], lambda m: 64 * (m % 16 // 8) + 16 * (m // 32) + 8 * (m % 32 // 16) + m % 8
    )
    couple = staggered(couple, 32)
    group = group[:16] // 2
    row = row[:16]
    for x2 in range(4):
        kept = jnp.where(group == (x2 + row) % 4, couple, 0.0)
        for g in range(4):
            piece = jnp.sum(jnp.where(row // 4 == g, kept, 0.0), axis=0, keepdims=True)
            out[8 * x2 + g, 6:7] = piece
            out[8 * x2 + 4 + g, 6:7] = piece
            out[8 * x2 + g, 7:8] = piece
            out[8 * x2 + 4 + g, 7:8] = piece

    copies[2].wait()
    products = jnp.zeros((64, 128), jnp.float32)
    for k in range(CHUNKS):
        copies[3 + 2 * k].wait()
        copies[4 + 2 * k].wait()
        products += lax.dot_general(
            two_parts(panel[k]), two_parts(solved_t[k]), NT, preferred_element_type=jnp.float32
        )
    total = products[:32] + products[32:]
    total = total[:, :64] + total[:, 64:]
    total = jnp.where(lax.axis_index("c") == 0, sketch[...], 0.0) - total
    for c2 in range(8):
        piece = packed(total[4 * c2 : 4 * c2 + 4])
        for x2 in range(4):
            out[8 * x2 + c2, 0:2] = piece


def split_body(got, out):
    x, c = lax.axis_index("x"), lax.axis_index("c")
    right = [unpacked(got[8 * k : 8 * k + 8, 0:2].sum(axis=0)) for k in range(4)]
    right = jnp.concatenate(
        [jnp.concatenate(right[:2], axis=0), jnp.concatenate(right[2:], axis=0)], axis=1
    )
    group = lax.broadcasted_iota(jnp.int32, (8, 128), 1) // 16
    row = lax.broadcasted_iota(jnp.int32, (8, 128), 0)

    mats = [jnp.zeros((8, 128), jnp.float32) for _ in range(4)]
    for c1 in range(8):
        piece = got[8 * x + c1, 2:6]
        piece = pltpu.roll(piece, (16 * (c1 + 8) - 16 * c) % 128, 1)
        for k in range(4):
            mats[k] = jnp.where(group == (c1 + row) % 8, piece[k : k + 1], mats[k])
    mats = [staggered(mat, -16) for mat in mats]

    halves = [jnp.zeros((8, 128), jnp.float32) for _ in range(2)]
    for a in range(2):
        for c1 in range(8):
            piece = got[8 * (c // 4 + 2 * a) + c1, 6:8]
            piece = pltpu.roll(piece, (16 * c1 + 128 - 32 * x) % 128, 1)[:1]
            for h in range(2):
                here = (group == (2 * row + h + c1) % 8) & (row // 4 == a)
                halves[h] = jnp.where(here, piece, halves[h])
    halves = [staggered(half, -32, -16 * h) for h, half in enumerate(halves)]

    own = got[pl.ds(pl.multiple_of(8 * x, 8), 8), 0:2].sum(axis=0)
    for h in range(2):
        near = jnp.concatenate([mats[h][:, :64], mats[2 + h][:, :64]], axis=1)
        far = jnp.concatenate([mats[h][:, 64:], mats[2 + h][:, 64:]], axis=1)
        near = jnp.where(lax.axis_index("zh") < 4, near, right)
        piece = own[:, 64 * h : 64 * h + 64]
        piece = jnp.concatenate([piece[0:1], piece[1:2]], axis=1)
        for k in range(8):
            for m, tile in enumerate((near, far, halves[h])):
                for j in range(8):
                    out[2 * k + h, 8 * m + j] = tile[j : j + 1]
            out[2 * k + h, 24] = piece


def applied(got, lanes, vector):
    terms = dot(got[:, 8:16, lanes].reshape(128, 64), vector[64:])
    near = dot(got[0:8, 0:8, lanes].reshape(64, 64), vector[:64])
    return jnp.concatenate([terms[:64] + near, terms[64:]], axis=0)


def last_body(got, out):
    right = unpacked(got[8:16, 0:8]).reshape(128, 64)
    terms = packed(applied(got, slice(0, 64), right))
    for k in range(8):
        out[k] = terms


def bent_body(parts, got, out, y_out):
    y_last = unpacked(parts[...].sum(axis=0))
    bent = dot(got[:, 16:24].reshape(128, 128), y_last).reshape(8, 2, 8, 64)
    bent = jnp.concatenate([bent[:, 0].reshape(64, 64), bent[:, 1].reshape(64, 64)], axis=1)

    x, h = lax.axis_index("x"), lax.axis_index("zl")
    row = lax.broadcasted_iota(jnp.int32, (8, 128), 0)
    half = lax.broadcasted_iota(jnp.int32, (8, 128), 1) // 64
    here = (half == x // 2) & (row // 2 == 2 * (x % 2) + h)
    rows = []
    for z in range(8):
        piece = got[z, 24:25]
        piece = jnp.where(row % 2 == x // 2, piece, pltpu.roll(piece, 64, 1))
        rows.append(jnp.where(here, piece, 0.0))
    terms = jnp.concatenate(rows, axis=0) - bent
    for k in range(8):
        out[k] = terms
    for g in range(4):
        y_out[g] = packed(y_last[32 * g : 32 * g + 32])


def first_body(parts, got, out):
    right = unpacked(parts[...].sum(axis=0).reshape(8, 8, 128)).reshape(128, 64)
    terms = applied(got, slice(64, 128), right)
    pieces = [packed(terms[32 * g : 32 * g + 32]) for g in range(4)]
    block = lax.axis_index("zh") % 4
    shown = pieces[0]
    for g in range(1, 4):
        shown = jnp.where(block == g, pieces[g], shown)
    for k in range(8):
        out[k, 0:16] = pieces[k % 4]
        out[k, 16:32] = shown


def own_body(parts, y_last, out):
    c, zh = lax.axis_index("c"), lax.axis_index("zh")
    total = parts[...].sum(axis=0)
    piece = jnp.where(c < 4, total[:16], y_last[c % 4])
    shown = jnp.where(zh < 4, total[16:], y_last[zh % 4])
    for k in range(8):
        out[k, 0:16] = piece
        half = k % 4 // 2
        out[k, 16:24] = shown[8 * half : 8 * half + 8]


def design_body(parts, design, out, held):
    for h in range(2):
        for x in range(4):
            piece = parts[4 * h + x, 0:16]
            for z in range(4):
                row = 64 * z + 16 * x + 8 * h
                held[row : row + 8, :] = piece[
                    8 * (z % 2) : 8 * (z % 2) + 8, 64 * (z // 2) : 64 * (z // 2) + 64
                ]
    turned = held[...].T.astype(jnp.bfloat16)
    for k in range(8):
        out[k] = lax.dot_general(
            turned, design[256 * k : 256 * k + 256], NT, preferred_element_type=jnp.float32
        )


def leverage_body(got, parts, prior_t, solution_rows, leverage):
    x, zl = lax.axis_index("x"), lax.axis_index("zl")
    for b in range(2):
        for h in range(2):
            piece = parts[4 * h + 2 * (x % 2) + b, 16:24]
            row = 16 * b + 8 * h
            solution_rows[row : row + 8, :] = jnp.where(zl == 0, piece[:, :64], piece[:, 64:])
    total = prior_t[...] + got[...].sum(axis=0)
    leverage[...] = jnp.sum(total * total, axis=0, keepdims=True) * (1.0 / 64)


def local(panel, solved, sketch, inverses, coupling, design, prior):
    message = call(
        start_body,
        f32(32, 8, 128),
        *(
            pltpu.with_memory_space_constraint(value, pltpu.HBM)
            for value in (panel, solved.T, sketch, inverses, coupling)
        ),
        specs=[pl.BlockSpec(memory_space=pl.ANY)] * 5,
        scratch=[
            pltpu.VMEM((2, 16, 128), jnp.float32),
            pltpu.VMEM((16, 128), jnp.float32),
            pltpu.VMEM((32, 64), jnp.float32),
            pltpu.VMEM((CHUNKS, 32, 4096 // CHUNKS), jnp.float32),
            pltpu.VMEM((CHUNKS, 64, 4096 // CHUNKS), jnp.float32),
            pltpu.SemaphoreType.DMA((3 + 2 * CHUNKS,)),
        ],
    )
    got = exchange(message, ("x", "c"))

    got = exchange(call(split_body, f32(16, 25, 1, 128), got), ("zh", "zl")).reshape(16, 25, 128)

    parts = exchange(call(last_body, f32(8, 64, 128), got), "c")

    bent, y_last = call(bent_body, (f32(8, 64, 128), f32(4, 16, 128)), parts, got)
    parts = exchange(bent, ("zl", "x"))

    parts = exchange(call(first_body, f32(8, 32, 128), parts, got), "c")
    parts = exchange(call(own_body, f32(8, 24, 128), parts, y_last), ("zl", "x"))

    message = call(
        design_body, f32(8, 64, 256), parts, design, scratch=[pltpu.VMEM((256, 64), jnp.float32)]
    )
    block_solution, leverage = call(
        leverage_body, (f32(32, 64), f32(1, 256)), exchange(message, "c"), parts, prior.T
    )
    return block_solution, leverage.reshape(256)


def solution(mesh):
    fine = Mesh(mesh.devices.reshape(8, 2, 4, 8), ("zh", "zl", "x", "c"))
    r = ("zh", "zl", "x")
    in_specs = (
        P(r, "c"),
        P("c", None),
        P(r, None),
        P(None, r, "c"),
        P(r, "c"),
        P(r, "c"),
        P((*r, "c"), None),
    )
    out_specs = (P(r, None), P((*r, "c")))
    return jax.shard_map(local, mesh=fine, in_specs=in_specs, out_specs=out_specs, check_vma=False)
```

```python
import jax
import jax.numpy as jnp
from jax import lax
from jax.experimental import pallas as pl
from jax.experimental.pallas import tpu as pltpu
from jax.sharding import Mesh
from jax.sharding import PartitionSpec as P

HIGHEST = lax.Precision.HIGHEST
VMEM = pl.BlockSpec(memory_space=pltpu.VMEM)
NT = (((1,), (1,)), ((), ()))
CHUNKS = 1


def dot(a, b):
    return jnp.dot(a, b, precision=HIGHEST, preferred_element_type=jnp.float32)


def exchange(value, axes):
    return lax.all_to_all(value, axes, 0, 0, tiled=True)


def packed(value):
    half = value.shape[-2] // 2
    return jnp.concatenate([value[..., :half, :], value[..., half:, :]], axis=-1)


def unpacked(value):
    return jnp.concatenate([value[..., :64], value[..., 64:]], axis=-2)


def call(body, out, *args, specs=None, scratch=(), limit=32 << 20):
    return pl.pallas_call(
        body,
        out_shape=out,
        in_specs=specs or [VMEM] * len(args),
        out_specs=jax.tree.map(lambda _: VMEM, out),
        scratch_shapes=scratch,
        compiler_params=pltpu.CompilerParams(vmem_limit_bytes=limit),
    )(*args)


def f32(*shape):
    return jax.ShapeDtypeStruct(shape, jnp.float32)


def two_parts(value):
    high = value.astype(jnp.bfloat16)
    low = (value - high.astype(jnp.float32)).astype(jnp.bfloat16)
    return jnp.concatenate([high, low], axis=0)


def permuted(value, source_of):
    row = lax.broadcasted_iota(jnp.int32, (128, 128), 0)
    lane = lax.broadcasted_iota(jnp.int32, (128, 128), 1)
    return dot(value, (row == source_of(lane)).astype(jnp.float32))


def staggered(value, step, shift=0):
    row = lax.broadcasted_iota(jnp.int32, value.shape, 0) % (128 // (step % 128 & -(step % 128)))
    out = value
    for i in range(128 // (step % 128 & -(step % 128))):
        turn = (shift + step * i) % 128
        out = jnp.where(row == i, pltpu.roll(value, turn, 1) if turn else value, out)
    return out


def start_body(panel_hbm, solved_hbm, sketch_hbm, inverses_hbm, coupling_hbm, out, *held):
    inverses, coupling, sketch, panel, solved_t, sems = held
    pairs = [(inverses_hbm, inverses), (coupling_hbm, coupling), (sketch_hbm, sketch)]
    for k in range(CHUNKS):
        span = pl.ds(k * (4096 // CHUNKS), 4096 // CHUNKS)
        pairs += [(solved_hbm.at[:, span], solved_t.at[k]), (panel_hbm.at[:, span], panel.at[k])]
    copies = [
        pltpu.make_async_copy(source, target, sems.at[k])
        for k, (source, target) in enumerate(pairs)
    ]
    for copy in copies:
        copy.start()

    copies[0].wait()
    both = jnp.concatenate([inverses[1], inverses[0]], axis=0)
    both = permuted(both, lambda m: 32 * (m % 16 // 4) + 4 * (m // 16) + m % 4)
    both = staggered(both, 16)
    group = lax.broadcasted_iota(jnp.int32, (32, 128), 1) // 16
    row = lax.broadcasted_iota(jnp.int32, (32, 128), 0)
    for c2 in range(8):
        kept = jnp.where(group == (c2 + row) % 8, both, 0.0)
        kept = kept.reshape(4, 8, 128).sum(axis=1)
        for x2 in range(4):
            for j in range(4):
                out[8 * x2 + c2, 2 + j] = kept[j : j + 1]

    copies[1].wait()
    couple = permuted(
        coupling[...], lambda m: 64 * (m % 16 // 8) + 16 * (m // 32) + 8 * (m % 32 // 16) + m % 8
    )
    couple = staggered(couple, 32)
    group = group[:16] // 2
    row = row[:16]
    for x2 in range(4):
        kept = jnp.where(group == (x2 + row) % 4, couple, 0.0)
        for g in range(4):
            piece = jnp.sum(jnp.where(row // 4 == g, kept, 0.0), axis=0, keepdims=True)
            out[8 * x2 + g, 6] = piece
            out[8 * x2 + 4 + g, 6] = piece

    copies[2].wait()
    products = jnp.zeros((64, 128), jnp.float32)
    for k in range(CHUNKS):
        copies[3 + 2 * k].wait()
        copies[4 + 2 * k].wait()
        products += lax.dot_general(
            two_parts(panel[k]), two_parts(solved_t[k]), NT, preferred_element_type=jnp.float32
        )
    total = products[:32] + products[32:]
    total = total[:, :64] + total[:, 64:]
    total = jnp.where(lax.axis_index("c") == 0, sketch[...], 0.0) - total
    for c2 in range(8):
        piece = packed(total[4 * c2 : 4 * c2 + 4])
        for x2 in range(4):
            out[8 * x2 + c2, 0] = piece[0:1]
            out[8 * x2 + c2, 1] = piece[1:2]


def split_body(got, out):
    x, c = lax.axis_index("x"), lax.axis_index("c")
    right = [unpacked(got[8 * k : 8 * k + 8, 0:2].sum(axis=0)) for k in range(4)]
    right = jnp.concatenate(
        [jnp.concatenate(right[:2], axis=0), jnp.concatenate(right[2:], axis=0)], axis=1
    )
    group = lax.broadcasted_iota(jnp.int32, (8, 128), 1) // 16
    row = lax.broadcasted_iota(jnp.int32, (8, 128), 0)

    mats = [jnp.zeros((8, 128), jnp.float32) for _ in range(4)]
    for c1 in range(8):
        piece = got[8 * x + c1, 2:6]
        piece = pltpu.roll(piece, (16 * (c1 + 8) - 16 * c) % 128, 1)
        for k in range(4):
            mats[k] = jnp.where(group == (c1 + row) % 8, piece[k : k + 1], mats[k])
    mats = [staggered(mat, -16) for mat in mats]

    halves = [jnp.zeros((8, 128), jnp.float32) for _ in range(2)]
    for a in range(2):
        for c1 in range(8):
            piece = got[8 * (c // 4 + 2 * a) + c1, 6:7]
            piece = pltpu.roll(piece, (16 * c1 + 128 - 32 * x) % 128, 1)[:1]
            for h in range(2):
                here = (group == (2 * row + h + c1) % 8) & (row // 4 == a)
                halves[h] = jnp.where(here, piece, halves[h])
    halves = [staggered(half, -32, -16 * h) for h, half in enumerate(halves)]

    own = got[pl.ds(pl.multiple_of(8 * x, 8), 8), 0:2].sum(axis=0)
    for h in range(2):
        near = jnp.concatenate([mats[h][:, :64], mats[2 + h][:, :64]], axis=1)
        far = jnp.concatenate([mats[h][:, 64:], mats[2 + h][:, 64:]], axis=1)
        near = jnp.where(lax.axis_index("zh") < 4, near, right)
        piece = own[:, 64 * h : 64 * h + 64]
        piece = jnp.concatenate([piece[0:1], piece[1:2]], axis=1)
        for k in range(8):
            for m, tile in enumerate((near, far, halves[h])):
                for j in range(8):
                    out[2 * k + h, 8 * m + j] = tile[j : j + 1]
            out[2 * k + h, 24] = piece


def applied(got, lanes, vector):
    terms = dot(got[:, 8:16, lanes].reshape(128, 64), vector[64:])
    near = dot(got[0:8, 0:8, lanes].reshape(64, 64), vector[:64])
    return jnp.concatenate([terms[:64] + near, terms[64:]], axis=0)


def last_body(got, out):
    right = unpacked(got[8:16, 0:8]).reshape(128, 64)
    terms = packed(applied(got, slice(0, 64), right))
    for k in range(8):
        out[k] = terms


def bent_body(parts, got, out, y_out):
    y_last = unpacked(parts[...].sum(axis=0))
    bent = dot(got[:, 16:24].reshape(128, 128), y_last).reshape(8, 2, 8, 64)
    bent = jnp.concatenate([bent[:, 0].reshape(64, 64), bent[:, 1].reshape(64, 64)], axis=1)

    x, h = lax.axis_index("x"), lax.axis_index("zl")
    row = lax.broadcasted_iota(jnp.int32, (8, 128), 0)
    half = lax.broadcasted_iota(jnp.int32, (8, 128), 1) // 64
    here = (half == x // 2) & (row // 2 == 2 * (x % 2) + h)
    rows = []
    for z in range(8):
        piece = got[z, 24:25]
        piece = jnp.where(row % 2 == x // 2, piece, pltpu.roll(piece, 64, 1))
        rows.append(jnp.where(here, piece, 0.0))
    terms = jnp.concatenate(rows, axis=0) - bent
    for k in range(8):
        out[k] = terms
    for g in range(4):
        y_out[g] = packed(y_last[32 * g : 32 * g + 32])


def first_body(parts, got, out):
    right = unpacked(parts[...].sum(axis=0).reshape(8, 8, 128)).reshape(128, 64)
    terms = applied(got, slice(64, 128), right)
    pieces = [packed(terms[32 * g : 32 * g + 32]) for g in range(4)]
    block = lax.axis_index("zh") % 4
    shown = pieces[0]
    for g in range(1, 4):
        shown = jnp.where(block == g, pieces[g], shown)
    for k in range(8):
        out[k, 0:16] = pieces[k % 4]
        out[k, 16:32] = shown


def own_body(parts, y_last, out):
    c, zh = lax.axis_index("c"), lax.axis_index("zh")
    total = parts[...].sum(axis=0)
    piece = jnp.where(c < 4, total[:16], y_last[c % 4])
    shown = jnp.where(zh < 4, total[16:], y_last[zh % 4])
    for k in range(8):
        out[k, 0:16] = piece
        half = k % 4 // 2
        out[k, 16:24] = shown[8 * half : 8 * half + 8]


def design_body(parts, design, out, held):
    for h in range(2):
        for x in range(4):
            piece = parts[4 * h + x, 0:16]
            for z in range(4):
                row = 64 * z + 16 * x + 8 * h
                held[row : row + 8, :] = piece[
                    8 * (z % 2) : 8 * (z % 2) + 8, 64 * (z // 2) : 64 * (z // 2) + 64
                ]
    turned = held[...].T.astype(jnp.bfloat16)
    for k in range(8):
        out[k] = lax.dot_general(
            turned, design[256 * k : 256 * k + 256], NT, preferred_element_type=jnp.float32
        )


def leverage_body(got, parts, prior_t, solution_rows, leverage):
    x, zl = lax.axis_index("x"), lax.axis_index("zl")
    for b in range(2):
        for h in range(2):
            piece = parts[4 * h + 2 * (x % 2) + b, 16:24]
            row = 16 * b + 8 * h
            solution_rows[row : row + 8, :] = jnp.where(zl == 0, piece[:, :64], piece[:, 64:])
    total = prior_t[...] + got[...].sum(axis=0)
    leverage[...] = jnp.sum(total * total, axis=0, keepdims=True) * (1.0 / 64)


def local(panel, solved, sketch, inverses, coupling, design, prior):
    message = call(
        start_body,
        f32(32, 7, 1, 128),
        *(
            pltpu.with_memory_space_constraint(value, pltpu.HBM)
            for value in (panel, solved.T, sketch, inverses, coupling)
        ),
        specs=[pl.BlockSpec(memory_space=pl.ANY)] * 5,
        scratch=[
            pltpu.VMEM((2, 16, 128), jnp.float32),
            pltpu.VMEM((16, 128), jnp.float32),
            pltpu.VMEM((32, 64), jnp.float32),
            pltpu.VMEM((CHUNKS, 32, 4096 // CHUNKS), jnp.float32),
            pltpu.VMEM((CHUNKS, 64, 4096 // CHUNKS), jnp.float32),
            pltpu.SemaphoreType.DMA((3 + 2 * CHUNKS,)),
        ],
    )
    got = exchange(message, ("x", "c")).reshape(32, 7, 128)

    got = exchange(call(split_body, f32(16, 25, 1, 128), got), ("zh", "zl")).reshape(16, 25, 128)

    parts = exchange(call(last_body, f32(8, 64, 128), got), "c")

    bent, y_last = call(bent_body, (f32(8, 64, 128), f32(4, 16, 128)), parts, got)
    parts = exchange(bent, ("zl", "x"))

    parts = exchange(call(first_body, f32(8, 32, 128), parts, got), "c")
    parts = exchange(call(own_body, f32(8, 24, 128), parts, y_last), ("zl", "x"))

    message = call(
        design_body, f32(8, 64, 256), parts, design, scratch=[pltpu.VMEM((256, 64), jnp.float32)]
    )
    block_solution, leverage = call(
        leverage_body, (f32(32, 64), f32(1, 256)), exchange(message, "c"), parts, prior.T
    )
    return block_solution, leverage.reshape(256)


def solution(mesh):
    fine = Mesh(mesh.devices.reshape(8, 2, 4, 8), ("zh", "zl", "x", "c"))
    r = ("zh", "zl", "x")
    in_specs = (
        P(r, "c"),
        P("c", None),
        P(r, None),
        P(None, r, "c"),
        P(r, "c"),
        P(r, "c"),
        P((*r, "c"), None),
    )
    out_specs = (P(r, None), P((*r, "c")))
    return jax.shard_map(local, mesh=fine, in_specs=in_specs, out_specs=out_specs, check_vma=False)
```
